128 devices in a mesh: seq: 32 (over z, y_hi, x), chan: 4 (over y_lo, core).
Axes of the slice: x: 4, y: 4 (y_hi: 2, y_lo: 2; y = y_hi * 2 + y_lo), z: 4, core: 2. Of those that a mesh axis runs over, the one named last changes fastest.
Arguments:
- query_proj: bfloat16 [128, 131072], P('chan', 'seq'), may hold values from -6 to 6
- key_proj: bfloat16 [128, 131072], P('chan', 'seq'), may hold values from -6 to 6
- value_proj: bfloat16 [128, 131072], P('chan', 'seq'), may hold values from -6 to 6
- out_cotangent: bfloat16 [128, 131072], P('chan', 'seq'), may hold values from -6 to 6
- filter_raw: float32 [32, 131072], P(None, 'seq'), may hold values from -6 to 6
Outputs:
- query_grad: bfloat16 [128, 131072], P('chan', 'seq')
- key_grad: bfloat16 [128, 131072], P('chan', 'seq')
- value_grad: bfloat16 [128, 131072], P('chan', 'seq')
- filter_grad: float32 [32, 131072], P('chan', 'seq')
The draws below stay inside these ranges and needn't reach their ends.
All inputs are finite; a program needn't handle non-finite values.
Results may differ from the reference program's by a relative error of at most 0.004.
Values sent between devices are 32-bit elements; how exact they have to be, the bound alone decides.
No kernel may reach another device: no remote copies, remote signals or barrier semaphores. Data moves between devices by JAX's collectives and lax.ppermute only.
A program may use at most 128 MiB of HBM per device.

```python
import math
import jax
import jax.numpy as jnp
from jax import lax

CH_DEV = 32
LENGTH = 131072
FFT_LEN = 262144
CHANNELS = 128
N_CHAN = 4


def level_of(key, dims, split, smallest, high):
    def one(dim, shards_of):
        steps = jax.random.uniform(jax.random.fold_in(jax.random.fold_in(key, 6), dim), (shards_of,), jnp.float32, smallest / len(split), high / len(split))
        return jnp.repeat(jnp.exp(steps), dims[dim] // shards_of).reshape((-1,) + (1,) * (len(dims) - dim - 1))

    gain = one(*split[0])
    for cut in split[1:]:
        gain = gain * one(*cut)
    return gain


def gaussian(rng, shape, scale, bound, pieces=(), held_as=jnp.bfloat16):
    drawn = jax.random.normal(rng, shape, jnp.float32) * scale
    if len(pieces) > 0:
        drawn = level_of(rng, shape, pieces, -0.22, 0.18) * drawn
    return jnp.clip(drawn, min=-bound, max=bound).astype(held_as)


def setup_inputs(seed: int = 0) -> dict:
    keys = jax.random.split(jax.random.key(seed), 6)
    query_proj = gaussian(keys[0], (CHANNELS, LENGTH), 1.0, 6.0, ((0, 4), (1, 32)))
    key_proj = gaussian(keys[1], (CHANNELS, LENGTH), 1.0, 6.0, ((0, 4), (1, 32)))
    value_proj = gaussian(keys[2], (CHANNELS, LENGTH), 1.0, 6.0, ((0, 4), (1, 32)))
    out_cotangent = gaussian(keys[3], (CHANNELS, LENGTH), 1.0, 6.0, ((0, 4), (1, 32)))
    filter_raw = gaussian(keys[4], (CH_DEV, LENGTH), 1.0, 6.0, ((1, 32),), jnp.float32)
    return dict(query_proj=query_proj, key_proj=key_proj, value_proj=value_proj, out_cotangent=out_cotangent, filter_raw=filter_raw)


def reference(query_proj, key_proj, value_proj, out_cotangent, filter_raw):
    gated = key_proj.astype(jnp.float32) * value_proj.astype(jnp.float32)
    carried = query_proj.astype(jnp.float32) * out_cotangent.astype(jnp.float32)
    scale = 1.0 / math.sqrt(LENGTH)
    filters = jnp.tile(filter_raw * scale, (N_CHAN, 1))
    gated_spec = jnp.fft.rfft(gated, n=FFT_LEN, axis=1)
    carried_spec = jnp.fft.rfft(carried, n=FFT_LEN, axis=1)
    filter_spec = jnp.fft.rfft(filters, n=FFT_LEN, axis=1)
    conv_out = jnp.fft.irfft(gated_spec * filter_spec, n=FFT_LEN, axis=1)[:, :LENGTH]
    adjoint = jnp.fft.irfft(carried_spec * jnp.conj(filter_spec), n=FFT_LEN, axis=1)[:, :LENGTH]
    slab_grad = jnp.fft.irfft(carried_spec * jnp.conj(gated_spec), n=FFT_LEN, axis=1)[:, :LENGTH]
    filter_grad = lax.optimization_barrier(jnp.sum(slab_grad.reshape(N_CHAN, CH_DEV, LENGTH), axis=0)) * scale
    query_grad = (conv_out * out_cotangent.astype(jnp.float32)).astype(jnp.bfloat16)
    key_grad = (adjoint * value_proj.astype(jnp.float32)).astype(jnp.bfloat16)
    value_grad = (adjoint * key_proj.astype(jnp.float32)).astype(jnp.bfloat16)
    return (query_grad, key_grad, value_grad, filter_grad.astype(jnp.float32))
```

```python
import math

import jax
import jax.numpy as jnp
import ml_dtypes
import numpy as np
from jax import lax
from jax.experimental import pallas as pl
from jax.experimental.pallas import tpu as pltpu
from jax.sharding import PartitionSpec as P

F32 = jnp.float32
BF16 = jnp.bfloat16
OUTER = 8
MIDDLE = 128
INNER = 128
SIGNALS = 3
VMEM_BYTES = 48 * 1024 * 1024


def halves(table):
    table = table.astype(np.float32)
    high = table.astype(ml_dtypes.bfloat16)
    low = (table - high.astype(np.float32)).astype(ml_dtypes.bfloat16)
    return high, low


def tables(scale):
    rows = OUTER * MIDDLE
    length = rows * INNER
    j = np.arange(OUTER)[:, None, None]
    k0 = np.arange(MIDDLE)[None, :, None]
    m0 = np.arange(MIDDLE)[None, None, :]
    angle = 2.0 * np.pi * m0 * (j + OUTER * k0 + 0.25) / rows
    cos, sin = np.cos(angle), np.sin(angle)
    mid = np.concatenate(
        [np.concatenate([cos, sin], axis=2), np.concatenate([-sin, cos], axis=2)], axis=1
    )
    mid_back = mid.transpose(0, 2, 1)
    l = np.arange(INNER)
    turn = 2.0 * np.pi * l[None, None, :] * (j + OUTER * k0 + 0.25) / length
    turn_table = np.stack([np.cos(turn), np.sin(turn)], axis=1).astype(np.float32)
    angle = 2.0 * np.pi * ((l[:, None] * l[None, :]) % INNER) / INNER
    cos, sin = np.cos(angle), np.sin(angle)
    last = np.concatenate(
        [np.concatenate([cos, -sin], axis=1), np.concatenate([sin, cos], axis=1)], axis=0
    )
    last_back = last.T * scale
    return (
        np.stack(halves(mid), axis=1),
        np.stack(halves(mid_back), axis=1),
        turn_table,
        np.stack(halves(last), axis=0),
        np.stack(halves(last_back), axis=0),
    )


def times(pair, cos, sin):
    return pair[0] * cos - pair[1] * sin, pair[1] * cos + pair[0] * sin


def add(first, second):
    return first[0] + second[0], first[1] + second[1]


def sub(first, second):
    return first[0] - second[0], first[1] - second[1]


def quarter(pair, sign):
    return (-pair[1], pair[0]) if sign > 0 else (pair[1], -pair[0])


def eighth(pair, sign):
    root = math.sqrt(0.5)
    if sign > 0:
        return (pair[0] - pair[1]) * root, (pair[0] + pair[1]) * root
    return (pair[0] + pair[1]) * root, (pair[1] - pair[0]) * root


def four_point(z, sign):
    s0, d0 = add(z[0], z[2]), sub(z[0], z[2])
    s1, d1 = add(z[1], z[3]), quarter(sub(z[1], z[3]), sign)
    return [add(s0, s1), add(d0, d1), sub(s0, s1), sub(d0, d1)]


def eight_point(z, sign):
    even = four_point([add(z[b], z[b + 4]) for b in range(4)], sign)
    odd = [sub(z[b], z[b + 4]) for b in range(4)]
    odd[1] = eighth(odd[1], sign)
    odd[2] = quarter(odd[2], sign)
    odd[3] = quarter(eighth(odd[3], sign), sign)
    odd = four_point(odd, sign)
    return [even[0], odd[0], even[1], odd[1], even[2], odd[2], even[3], odd[3]]


def split(value):
    high = value.astype(BF16)
    return high, (value - high.astype(F32)).astype(BF16)


def dot(first, second):
    return jnp.dot(first, second, preferred_element_type=F32)


def table_first(table, data):
    high, low = split(data)
    return dot(table[0], high) + dot(table[0], low) + dot(table[1], high)


def table_last(data, table):
    high, low = split(data)
    return dot(high, table[0]) + dot(low, table[0]) + dot(high, table[1])


def convolve_kernel(
    x_ref, mid_ref, mid_back_ref, turn_ref, last_ref, last_back_ref, y_ref, first_ref, final_ref
):
    blocks, _, block_rows, _ = x_ref.shape
    per = blocks // OUTER
    chunk = 16
    shift = [(math.cos(math.pi * b / 16), math.sin(math.pi * b / 16)) for b in range(OUTER)]

    def opening(step, carry):
        row = step * chunk
        inner_block = row // block_rows
        start = pl.multiple_of(row % block_rows, chunk)
        row = pl.multiple_of(row, chunk)
        for a in range(SIGNALS):
            z = []
            for b in range(OUTER):
                value = x_ref[b * per + inner_block, a, pl.ds(start, chunk), :]
                cos, sin = shift[b]
                z.append((value * cos, value * (-sin)))
            z = eight_point(z, -1)
            for j in range(OUTER):
                for part in range(2):
                    high, low = split(z[j][part])
                    columns = slice(a * INNER, (a + 1) * INNER)
                    first_ref[j, 0, pl.ds(part * MIDDLE + row, chunk), columns] = high
                    first_ref[j, 1, pl.ds(part * MIDDLE + row, chunk), columns] = low
        return carry

    lax.fori_loop(0, MIDDLE // chunk, opening, 0)

    last = (last_ref[0], last_ref[1])
    last_back = (last_back_ref[0], last_back_ref[1])

    def body(j, carry):
        high, low = first_ref[j, 0], first_ref[j, 1]
        table = (mid_ref[j, 0], mid_ref[j, 1])
        mixed = dot(table[0], high) + dot(table[0], low) + dot(table[1], high)
        cos, sin = turn_ref[j, 0], turn_ref[j, 1]
        spectra = []
        for a in range(SIGNALS):
            columns = slice(a * INNER, (a + 1) * INNER)
            real, imag = times((mixed[:MIDDLE, columns], mixed[MIDDLE:, columns]), cos, -sin)
            out = table_last(jnp.concatenate([real, imag], axis=1), last)
            spectra.append((out[:, :INNER], out[:, INNER:]))
        gated, carried, filters = spectra
        products = (
            times(gated, filters[0], filters[1]),
            times(carried, filters[0], -filters[1]),
            times(carried, gated[0], -gated[1]),
        )
        reals, imags = [], []
        for a in range(SIGNALS):
            out = table_last(jnp.concatenate(products[a], axis=1), last_back)
            real, imag = times((out[:, :INNER], out[:, INNER:]), cos, sin)
            reals.append(real)
            imags.append(imag)
        stacked = jnp.concatenate(
            [jnp.concatenate(reals, axis=1), jnp.concatenate(imags, axis=1)], axis=0
        )
        final_ref[j] = table_first((mid_back_ref[j, 0], mid_back_ref[j, 1]), stacked)
        return carry

    lax.fori_loop(0, OUTER, body, 0)

    rows = 8

    def closing(step, carry):
        row = step * rows
        inner_block = row // block_rows
        start = pl.multiple_of(row % block_rows, rows)
        row = pl.multiple_of(row, rows)
        for a in range(SIGNALS):
            columns = slice(a * INNER, (a + 1) * INNER)
            z = [
                (
                    final_ref[j, pl.ds(row, rows), columns],
                    final_ref[j, pl.ds(MIDDLE + row, rows), columns],
                )
                for j in range(OUTER)
            ]
            z = eight_point(z, 1)
            for b in range(OUTER):
                cos, sin = shift[b]
                y_ref[b * per + inner_block, a, pl.ds(start, rows), :] = z[b][0] * cos - z[b][1] * sin
        return carry

    lax.fori_loop(0, MIDDLE // rows, closing, 0)


def in_vmem(count):
    return [pl.BlockSpec(memory_space=pltpu.VMEM)] * count


def convolve(received, scale):
    constants = [jnp.asarray(table) for table in tables(scale)]
    return pl.pallas_call(
        convolve_kernel,
        out_shape=jax.ShapeDtypeStruct(received.shape, F32),
        in_specs=in_vmem(6),
        out_specs=pl.BlockSpec(memory_space=pltpu.VMEM),
        scratch_shapes=[
            pltpu.VMEM((OUTER, 2, 2 * MIDDLE, SIGNALS * INNER), BF16),
            pltpu.VMEM((OUTER, 2 * MIDDLE, SIGNALS * INNER), F32),
        ],
        compiler_params=pltpu.CompilerParams(vmem_limit_bytes=VMEM_BYTES),
        name="convolve",
    )(received, *constants)


def shards(query_proj, key_proj, value_proj, out_cotangent, filter_raw):
    slab, width = query_proj.shape
    parts = lax.axis_size("seq")
    length = parts * width
    scale = 1.0 / (length * math.sqrt(length))
    key_float = key_proj.astype(F32)
    value_float = value_proj.astype(F32)
    cotangent_float = out_cotangent.astype(F32)
    gated = key_float * value_float
    carried = query_proj.astype(F32) * cotangent_float
    sent = jnp.stack([gated, carried, filter_raw], axis=1)
    sent = sent.reshape(slab, SIGNALS, width // INNER, INNER)
    received = lax.all_to_all(sent, "seq", split_axis=0, concat_axis=0, tiled=True)
    signals = convolve(received, scale)
    back = lax.all_to_all(signals, "seq", split_axis=0, concat_axis=0, tiled=True)
    filter_grad = lax.psum_scatter(back[:, 2], "chan", scatter_dimension=0, tiled=True)
    conv_out = back[:, 0].reshape(slab, width)
    adjoint = back[:, 1].reshape(slab, width)
    query_grad = (conv_out * cotangent_float).astype(BF16)
    key_grad = (adjoint * value_float).astype(BF16)
    value_grad = (adjoint * key_float).astype(BF16)
    return (query_grad, key_grad, value_grad, filter_grad.reshape(-1, width))


def solution(mesh):
    placed = (
        P("chan", "seq"),
        P("chan", "seq"),
        P("chan", "seq"),
        P("chan", "seq"),
        P(None, "seq"),
    )
    return jax.shard_map(
        shards,
        mesh=mesh,
        in_specs=placed,
        out_specs=(P("chan", "seq"), P("chan", "seq"), P("chan", "seq"), P("chan", "seq")),
        check_vma=False,
    )
```

```python
import math

import jax
import jax.numpy as jnp
import ml_dtypes
import numpy as np
from jax import lax
from jax.experimental import pallas as pl
from jax.experimental.pallas import tpu as pltpu
from jax.sharding import PartitionSpec as P

F32 = jnp.float32
BF16 = jnp.bfloat16
OUTER = 8
MIDDLE = 128
INNER = 128
SIGNALS = 3
VMEM_BYTES = 48 * 1024 * 1024


def halves(table):
    table = table.astype(np.float32)
    high = table.astype(ml_dtypes.bfloat16)
    low = (table - high.astype(np.float32)).astype(ml_dtypes.bfloat16)
    return high, low


def tables(scale):
    rows = OUTER * MIDDLE
    length = rows * INNER
    j = np.arange(OUTER)[:, None, None]
    k0 = np.arange(MIDDLE)[None, :, None]
    m0 = np.arange(MIDDLE)[None, None, :]
    angle = 2.0 * np.pi * m0 * (j + OUTER * k0 + 0.25) / rows
    cos, sin = np.cos(angle), np.sin(angle)
    mid = np.concatenate(
        [np.concatenate([cos, sin], axis=2), np.concatenate([-sin, cos], axis=2)], axis=1
    )
    mid_back = mid.transpose(0, 2, 1)
    l = np.arange(INNER)
    turn = 2.0 * np.pi * l[None, None, :] * (j + OUTER * k0 + 0.25) / length
    turn_table = np.stack([np.cos(turn), np.sin(turn)], axis=1).astype(np.float32)
    angle = 2.0 * np.pi * ((l[:, None] * l[None, :]) % INNER) / INNER
    cos, sin = np.cos(angle), np.sin(angle)
    last = np.concatenate(
        [np.concatenate([cos, -sin], axis=1), np.concatenate([sin, cos], axis=1)], axis=0
    )
    last_back = last.T * scale
    return (
        np.stack(halves(mid), axis=1),
        np.stack(halves(mid_back), axis=1),
        turn_table,
        np.stack(halves(last), axis=0),
        np.stack(halves(last_back), axis=0),
    )


def times(pair, cos, sin):
    return pair[0] * cos - pair[1] * sin, pair[1] * cos + pair[0] * sin


def add(first, second):
    return first[0] + second[0], first[1] + second[1]


def sub(first, second):
    return first[0] - second[0], first[1] - second[1]


def quarter(pair, sign):
    return (-pair[1], pair[0]) if sign > 0 else (pair[1], -pair[0])


def eighth(pair, sign):
    root = math.sqrt(0.5)
    if sign > 0:
        return (pair[0] - pair[1]) * root, (pair[0] + pair[1]) * root
    return (pair[0] + pair[1]) * root, (pair[1] - pair[0]) * root


def four_point(z, sign):
    s0, d0 = add(z[0], z[2]), sub(z[0], z[2])
    s1, d1 = add(z[1], z[3]), quarter(sub(z[1], z[3]), sign)
    return [add(s0, s1), add(d0, d1), sub(s0, s1), sub(d0, d1)]


def eight_point(z, sign):
    even = four_point([add(z[b], z[b + 4]) for b in range(4)], sign)
    odd = [sub(z[b], z[b + 4]) for b in range(4)]
    odd[1] = eighth(odd[1], sign)
    odd[2] = quarter(odd[2], sign)
    odd[3] = quarter(eighth(odd[3], sign), sign)
    odd = four_point(odd, sign)
    return [even[0], odd[0], even[1], odd[1], even[2], odd[2], even[3], odd[3]]


def split(value):
    high = value.astype(BF16)
    return high, (value - high.astype(F32)).astype(BF16)


def dot(first, second):
    return jnp.dot(first, second, preferred_element_type=F32)


def table_first(table, data):
    high, low = split(data)
    return dot(table[0], high) + dot(table[0], low) + dot(table[1], high)


def table_last(data, table):
    high, low = split(data)
    return dot(high, table[0]) + dot(low, table[0]) + dot(high, table[1])


def convolve_kernel(
    x_ref, mid_ref, mid_back_ref, turn_ref, last_ref, last_back_ref, y_ref, first_ref, final_ref
):
    blocks, _, block_rows, _ = x_ref.shape
    per = blocks // OUTER
    chunk = 16
    shift = [(math.cos(math.pi * b / 16), math.sin(math.pi * b / 16)) for b in range(OUTER)]

    def opening(step, carry):
        row = step * chunk
        inner_block = row // block_rows
        start = pl.multiple_of(row % block_rows, chunk)
        row = pl.multiple_of(row, chunk)
        for a in range(SIGNALS):
            z = []
            for b in range(OUTER):
                value = x_ref[b * per + inner_block, a, pl.ds(start, chunk), :]
                cos, sin = shift[b]
                z.append((value * cos, value * (-sin)))
            z = eight_point(z, -1)
            for j in range(OUTER):
                for part in range(2):
                    high, low = split(z[j][part])
                    columns = slice(a * INNER, (a + 1) * INNER)
                    first_ref[j, 0, pl.ds(part * MIDDLE + row, chunk), columns] = high
                    first_ref[j, 1, pl.ds(part * MIDDLE + row, chunk), columns] = low
        return carry

    lax.fori_loop(0, MIDDLE // chunk, opening, 0)

    last = (last_ref[0], last_ref[1])
    last_back = (last_back_ref[0], last_back_ref[1])

    def body(j, carry):
        high, low = first_ref[j, 0], first_ref[j, 1]
        table = (mid_ref[j, 0], mid_ref[j, 1])
        mixed = dot(table[0], high) + dot(table[0], low) + dot(table[1], high)
        cos, sin = turn_ref[j, 0], turn_ref[j, 1]
        spectra = []
        for a in range(SIGNALS):
            columns = slice(a * INNER, (a + 1) * INNER)
            real, imag = times((mixed[:MIDDLE, columns], mixed[MIDDLE:, columns]), cos, -sin)
            out = table_last(jnp.concatenate([real, imag], axis=1), last)
            spectra.append((out[:, :INNER], out[:, INNER:]))
        gated, carried, filters = spectra
        products = (
            times(gated, filters[0], filters[1]),
            times(carried, filters[0], -filters[1]),
            times(carried, gated[0], -gated[1]),
        )
        reals, imags = [], []
        for a in range(SIGNALS):
            out = table_last(jnp.concatenate(products[a], axis=1), last_back)
            real, imag = times((out[:, :INNER], out[:, INNER:]), cos, sin)
            reals.append(real)
            imags.append(imag)
        stacked = jnp.concatenate(
            [jnp.concatenate(reals, axis=1), jnp.concatenate(imags, axis=1)], axis=0
        )
        final_ref[j] = table_first((mid_back_ref[j, 0], mid_back_ref[j, 1]), stacked)
        return carry

    lax.fori_loop(0, OUTER, body, 0)

    rows = 8

    def closing(step, carry):
        row = step * rows
        inner_block = row // block_rows
        start = pl.multiple_of(row % block_rows, rows)
        row = pl.multiple_of(row, rows)
        for a in range(SIGNALS):
            columns = slice(a * INNER, (a + 1) * INNER)
            z = [
                (
                    final_ref[j, pl.ds(row, rows), columns],
                    final_ref[j, pl.ds(MIDDLE + row, rows), columns],
                )
                for j in range(OUTER)
            ]
            z = eight_point(z, 1)
            for b in range(OUTER):
                cos, sin = shift[b]
                y_ref[b * per + inner_block, a, pl.ds(start, rows), :] = z[b][0] * cos - z[b][1] * sin
        return carry

    lax.fori_loop(0, MIDDLE // rows, closing, 0)


def in_vmem(count):
    return [pl.BlockSpec(memory_space=pltpu.VMEM)] * count


def convolve(received, scale):
    constants = [jnp.asarray(table) for table in tables(scale)]
    return pl.pallas_call(
        convolve_kernel,
        out_shape=jax.ShapeDtypeStruct(received.shape, F32),
        in_specs=in_vmem(6),
        out_specs=pl.BlockSpec(memory_space=pltpu.VMEM),
        scratch_shapes=[
            pltpu.VMEM((OUTER, 2, 2 * MIDDLE, SIGNALS * INNER), BF16),
            pltpu.VMEM((OUTER, 2 * MIDDLE, SIGNALS * INNER), F32),
        ],
        compiler_params=pltpu.CompilerParams(vmem_limit_bytes=VMEM_BYTES),
        name="convolve",
    )(received, *constants)


def shards(query_proj, key_proj, value_proj, out_cotangent, filter_raw):
    slab, width = query_proj.shape
    parts = lax.axis_size("seq")
    length = parts * width
    scale = 1.0 / (length * math.sqrt(length))
    key_float = key_proj.astype(F32)
    value_float = value_proj.astype(F32)
    cotangent_float = out_cotangent.astype(F32)
    gated = key_float * value_float
    carried = query_proj.astype(F32) * cotangent_float
    sent = jnp.stack([gated, carried, filter_raw], axis=1)
    sent = sent.reshape(slab, SIGNALS, width // INNER, INNER)
    received = lax.all_to_all(sent, "seq", split_axis=0, concat_axis=0, tiled=True)
    signals = convolve(received, scale)
    back = lax.all_to_all(signals, "seq", split_axis=0, concat_axis=0, tiled=True)
    groups = lax.axis_size("chan")
    rows = back[:, 2].reshape(groups, slab // groups, width // INNER, INNER)
    rows = lax.all_to_all(rows, "chan", split_axis=0, concat_axis=0, tiled=True)
    filter_grad = jnp.sum(rows, axis=0)
    conv_out = back[:, 0].reshape(slab, width)
    adjoint = back[:, 1].reshape(slab, width)
    query_grad = (conv_out * cotangent_float).astype(BF16)
    key_grad = (adjoint * value_float).astype(BF16)
    value_grad = (adjoint * key_float).astype(BF16)
    return (query_grad, key_grad, value_grad, filter_grad.reshape(-1, width))


def solution(mesh):
    placed = (
        P("chan", "seq"),
        P("chan", "seq"),
        P("chan", "seq"),
        P("chan", "seq"),
        P(None, "seq"),
    )
    return jax.shard_map(
        shards,
        mesh=mesh,
        in_specs=placed,
        out_specs=(P("chan", "seq"), P("chan", "seq"), P("chan", "seq"), P("chan", "seq")),
        check_vma=False,
    )
```

```python
import math

import jax
import jax.numpy as jnp
import ml_dtypes
import numpy as np
from jax import lax
from jax.experimental import pallas as pl
from jax.experimental.pallas import tpu as pltpu
from jax.sharding import PartitionSpec as P

F32 = jnp.float32
BF16 = jnp.bfloat16
SIGNALS = 3
ROWS = 256
TURNS = 4
INNER = 128
CHUNK = 16
VMEM_BYTES = 28 * 1024 * 1024


def halves(table):
    table = table.astype(np.float32)
    high = table.astype(ml_dtypes.bfloat16)
    low = (table - high.astype(np.float32)).astype(ml_dtypes.bfloat16)
    return np.stack([high, low])


def tables(scale):
    width = TURNS * INNER
    k = np.arange(ROWS)[:, None] + 0.25
    angle = 2.0 * np.pi * k * np.arange(ROWS)[None, :] / ROWS
    first = np.concatenate([np.cos(angle), -np.sin(angle)], axis=0)
    turn = 2.0 * np.pi * k * np.arange(width)[None, :] / (ROWS * width)
    turn = np.stack([np.cos(turn), np.sin(turn)]).astype(np.float32)
    l = np.arange(INNER)
    lasts = []
    for j in range(TURNS):
        angle = 2.0 * np.pi * (l[:, None] * (j + TURNS * l[None, :]) % width) / width
        cos, sin = np.cos(angle), np.sin(angle)
        lasts.append(
            np.concatenate(
                [np.concatenate([cos, -sin], axis=1), np.concatenate([sin, cos], axis=1)], axis=0
            )
        )
    last = np.stack(lasts)
    return (
        halves(first),
        halves(first.T),
        turn,
        halves(last),
        halves(last.transpose(0, 2, 1) * scale),
    )


def times(pair, cos, sin):
    return pair[0] * cos - pair[1] * sin, pair[1] * cos + pair[0] * sin


def add(first, second):
    return first[0] + second[0], first[1] + second[1]


def sub(first, second):
    return first[0] - second[0], first[1] - second[1]


def quarter(pair, sign):
    return (-pair[1], pair[0]) if sign > 0 else (pair[1], -pair[0])


def four_point(z, sign):
    s0, d0 = add(z[0], z[2]), sub(z[0], z[2])
    s1, d1 = add(z[1], z[3]), sub(z[1], z[3])
    if sign > 0:
        return [
            add(s0, s1),
            (d0[0] - d1[1], d0[1] + d1[0]),
            sub(s0, s1),
            (d0[0] + d1[1], d0[1] - d1[0]),
        ]
    return [
        add(s0, s1),
        (d0[0] + d1[1], d0[1] - d1[0]),
        sub(s0, s1),
        (d0[0] - d1[1], d0[1] + d1[0]),
    ]


def split(value):
    high = value.astype(BF16)
    return high, (value - high.astype(F32)).astype(BF16)


def dot(first, second):
    return jnp.dot(first, second, preferred_element_type=F32)


def lanes(index):
    return slice(index * INNER, (index + 1) * INNER)


def convolve_kernel(
    x_ref,
    first_ref,
    first_back_ref,
    turn_ref,
    last_ref,
    last_back_ref,
    y_ref,
    mixed_ref,
    z_ref,
    spectra_ref,
    product_ref,
    u_ref,
    v_ref,
):
    blocks, _, _, block_rows, _ = x_ref.shape
    chunks = [slice(i, i + CHUNK) for i in range(0, ROWS, CHUNK)]

    for a in (2, 0, 1):
        for pair in range(TURNS // 2):
            data = jnp.concatenate(
                [x_ref[:, a, 2 * pair + p].reshape(ROWS, INNER) for p in range(2)], axis=1
            )
            high, low = split(data)
            mixed_ref[a, :, slice(2 * pair * INNER, 2 * (pair + 1) * INNER)] = (
                dot(first_ref[0], high) + dot(first_ref[0], low) + dot(first_ref[1], high)
            )
        for rows in chunks:
            imag_rows = slice(ROWS + rows.start, ROWS + rows.stop)
            z = []
            for p in range(TURNS):
                cos, sin = turn_ref[0, rows, lanes(p)], turn_ref[1, rows, lanes(p)]
                pair = (mixed_ref[a, rows, lanes(p)], mixed_ref[a, imag_rows, lanes(p)])
                z.append(times(pair, cos, -sin))
            z = four_point(z, -1)
            for j in range(TURNS):
                for part in range(2):
                    high, low = split(z[j][part])
                    z_ref[0, j, a, rows, lanes(part)] = high
                    z_ref[1, j, a, rows, lanes(part)] = low

    for j in range(TURNS):
        for a in (2, 0, 1):
            high, low = z_ref[0, j, a], z_ref[1, j, a]
            spectra_ref[j, a] = (
                dot(high, last_ref[0, j]) + dot(low, last_ref[0, j]) + dot(high, last_ref[1, j])
            )
        for rows in chunks:
            gated, carried, filters = [
                (spectra_ref[j, a, rows, lanes(0)], spectra_ref[j, a, rows, lanes(1)])
                for a in range(SIGNALS)
            ]
            products = (
                times(gated, filters[0], filters[1]),
                times(carried, filters[0], -filters[1]),
                times(carried, gated[0], -gated[1]),
            )
            for a in range(SIGNALS):
                for part in range(2):
                    product_ref[j, a, rows, lanes(part)] = products[a][part].astype(BF16)
        for a in range(SIGNALS):
            data = product_ref[j, a]
            u_ref[j, a] = dot(data, last_back_ref[0, j]) + dot(data, last_back_ref[1, j])

    for a in range(SIGNALS):
        for rows in chunks:
            imag_rows = slice(ROWS + rows.start, ROWS + rows.stop)
            z = [(u_ref[j, a, rows, lanes(0)], u_ref[j, a, rows, lanes(1)]) for j in range(TURNS)]
            z = four_point(z, 1)
            for p in range(TURNS):
                cos, sin = turn_ref[0, rows, lanes(p)], turn_ref[1, rows, lanes(p)]
                real, imag = times(z[p], cos, sin)
                v_ref[a, rows, lanes(p)] = real.astype(BF16)
                v_ref[a, imag_rows, lanes(p)] = imag.astype(BF16)
        for pair in range(TURNS // 2):
            data = v_ref[a, :, slice(2 * pair * INNER, 2 * (pair + 1) * INNER)]
            out = dot(first_back_ref[0], data) + dot(first_back_ref[1], data)
            for p in range(2):
                y_ref[:, a, 2 * pair + p] = out[:, lanes(p)].reshape(blocks, block_rows, INNER)


def in_vmem(count):
    return [pl.BlockSpec(memory_space=pltpu.VMEM)] * count


def convolve(received, scale):
    constants = [jnp.asarray(table) for table in tables(scale)]
    width = TURNS * INNER
    return pl.pallas_call(
        convolve_kernel,
        out_shape=jax.ShapeDtypeStruct(received.shape, F32),
        in_specs=in_vmem(6),
        out_specs=pl.BlockSpec(memory_space=pltpu.VMEM),
        scratch_shapes=[
            pltpu.VMEM((SIGNALS, 2 * ROWS, width), F32),
            pltpu.VMEM((2, TURNS, SIGNALS, ROWS, 2 * INNER), BF16),
            pltpu.VMEM((TURNS, SIGNALS, ROWS, 2 * INNER), F32),
            pltpu.VMEM((TURNS, SIGNALS, ROWS, 2 * INNER), BF16),
            pltpu.VMEM((TURNS, SIGNALS, ROWS, 2 * INNER), F32),
            pltpu.VMEM((SIGNALS, 2 * ROWS, width), BF16),
        ],
        compiler_params=pltpu.CompilerParams(vmem_limit_bytes=VMEM_BYTES),
        name="convolve",
    )(received, *constants)


def shards(query_proj, key_proj, value_proj, out_cotangent, filter_raw):
    slab, width = query_proj.shape
    parts = lax.axis_size("seq")
    groups = lax.axis_size("chan")
    length = parts * width
    scale = 1.0 / (length * math.sqrt(length))
    block_rows = ROWS // parts
    key_float = key_proj.astype(F32)
    value_float = value_proj.astype(F32)
    cotangent_float = out_cotangent.astype(F32)
    gated = key_float * value_float
    carried = query_proj.astype(F32) * cotangent_float
    sent = jnp.stack([gated, carried, filter_raw], axis=1)
    sent = sent.reshape(slab, SIGNALS, block_rows, TURNS, INNER).transpose(0, 1, 3, 2, 4)
    received = lax.all_to_all(sent, "seq", split_axis=0, concat_axis=0, tiled=True)
    signals = convolve(received, scale)
    back = lax.all_to_all(signals, "seq", split_axis=0, concat_axis=0, tiled=True)
    rows = back[:, 2].reshape(groups, slab // groups, TURNS, block_rows, INNER)
    rows = lax.all_to_all(rows, "chan", split_axis=0, concat_axis=0, tiled=True)
    filter_grad = jnp.sum(rows, axis=0).transpose(0, 2, 1, 3).reshape(-1, width)
    back = back.transpose(0, 1, 3, 2, 4)
    conv_out = back[:, 0].reshape(slab, width)
    adjoint = back[:, 1].reshape(slab, width)
    query_grad = (conv_out * cotangent_float).astype(BF16)
    key_grad = (adjoint * value_float).astype(BF16)
    value_grad = (adjoint * key_float).astype(BF16)
    return (query_grad, key_grad, value_grad, filter_grad)


def solution(mesh):
    placed = (
        P("chan", "seq"),
        P("chan", "seq"),
        P("chan", "seq"),
        P("chan", "seq"),
        P(None, "seq"),
    )
    return jax.shard_map(
        shards,
        mesh=mesh,
        in_specs=placed,
        out_specs=(P("chan", "seq"), P("chan", "seq"), P("chan", "seq"), P("chan", "seq")),
        check_vma=False,
    )
```

```python
import functools
import math

import jax
import jax.numpy as jnp
import ml_dtypes
import numpy as np
from jax import lax
from jax.experimental import pallas as pl
from jax.experimental.pallas import tpu as pltpu
from jax.sharding import PartitionSpec as P

F32 = jnp.float32
BF16 = jnp.bfloat16
SIGNALS = 3
ROWS = 256
TURNS = 4
INNER = 128
CHUNK = 16
GROUP = 8
VMEM_BYTES = 28 * 1024 * 1024


def halves(table):
    table = table.astype(np.float32)
    high = table.astype(ml_dtypes.bfloat16)
    low = (table - high.astype(np.float32)).astype(ml_dtypes.bfloat16)
    return np.stack([high, low])


def tables(scale):
    width = TURNS * INNER
    k = np.arange(ROWS)[:, None] + 0.25
    angle = 2.0 * np.pi * k * np.arange(ROWS)[None, :] / ROWS
    first = np.concatenate([np.cos(angle), -np.sin(angle)], axis=0)
    turn = 2.0 * np.pi * k * np.arange(width)[None, :] / (ROWS * width)
    turn = np.stack([np.cos(turn), np.sin(turn)]).astype(np.float32)
    l = np.arange(INNER)
    lasts = []
    for j in range(TURNS):
        angle = 2.0 * np.pi * (l[:, None] * (j + TURNS * l[None, :]) % width) / width
        cos, sin = np.cos(angle), np.sin(angle)
        lasts.append(
            np.concatenate(
                [np.concatenate([cos, -sin], axis=1), np.concatenate([sin, cos], axis=1)], axis=0
            )
        )
    last = np.stack(lasts)
    return (
        halves(first),
        halves(first.T),
        turn,
        halves(last),
        halves(last.transpose(0, 2, 1) * scale),
    )


def times(pair, cos, sin):
    return pair[0] * cos - pair[1] * sin, pair[1] * cos + pair[0] * sin


def add(first, second):
    return first[0] + second[0], first[1] + second[1]


def sub(first, second):
    return first[0] - second[0], first[1] - second[1]


def quarter(pair, sign):
    return (-pair[1], pair[0]) if sign > 0 else (pair[1], -pair[0])


def four_point(z, sign):
    s0, d0 = add(z[0], z[2]), sub(z[0], z[2])
    s1, d1 = add(z[1], z[3]), sub(z[1], z[3])
    if sign > 0:
        return [
            add(s0, s1),
            (d0[0] - d1[1], d0[1] + d1[0]),
            sub(s0, s1),
            (d0[0] + d1[1], d0[1] - d1[0]),
        ]
    return [
        add(s0, s1),
        (d0[0] + d1[1], d0[1] - d1[0]),
        sub(s0, s1),
        (d0[0] - d1[1], d0[1] + d1[0]),
    ]


def split(value):
    high = value.astype(BF16)
    return high, (value - high.astype(F32)).astype(BF16)


def dot(first, second):
    return jnp.dot(first, second, preferred_element_type=F32)


def lanes(index):
    return slice(index * INNER, (index + 1) * INNER)


def convolve_kernel(
    x_ref,
    first_ref,
    first_back_ref,
    turn_ref,
    last_ref,
    last_back_ref,
    y_ref,
    mixed_ref,
    z_ref,
    spectra_ref,
    product_ref,
    u_ref,
    v_ref,
):
    blocks, _, _, block_rows, _ = x_ref.shape
    chunks = [slice(i, i + CHUNK) for i in range(0, ROWS, CHUNK)]

    for a in (2, 0, 1):
        for pair in range(TURNS // 2):
            data = jnp.concatenate(
                [x_ref[:, a, 2 * pair + p].reshape(ROWS, INNER) for p in range(2)], axis=1
            )
            high, low = split(data)
            mixed_ref[a, :, slice(2 * pair * INNER, 2 * (pair + 1) * INNER)] = (
                dot(first_ref[0], high) + dot(first_ref[0], low) + dot(first_ref[1], high)
            )
        for rows in chunks:
            imag_rows = slice(ROWS + rows.start, ROWS + rows.stop)
            z = []
            for p in range(TURNS):
                cos, sin = turn_ref[0, rows, lanes(p)], turn_ref[1, rows, lanes(p)]
                pair = (mixed_ref[a, rows, lanes(p)], mixed_ref[a, imag_rows, lanes(p)])
                z.append(times(pair, cos, -sin))
            z = four_point(z, -1)
            for j in range(TURNS):
                for part in range(2):
                    high, low = split(z[j][part])
                    z_ref[0, j, a, rows, lanes(part)] = high
                    z_ref[1, j, a, rows, lanes(part)] = low

    for j in range(TURNS):
        for a in (2, 0, 1):
            high, low = z_ref[0, j, a], z_ref[1, j, a]
            spectra_ref[j, a] = (
                dot(high, last_ref[0, j]) + dot(low, last_ref[0, j]) + dot(high, last_ref[1, j])
            )
        for rows in chunks:
            gated, carried, filters = [
                (spectra_ref[j, a, rows, lanes(0)], spectra_ref[j, a, rows, lanes(1)])
                for a in range(SIGNALS)
            ]
            products = (
                times(gated, filters[0], filters[1]),
                times(carried, filters[0], -filters[1]),
                times(carried, gated[0], -gated[1]),
            )
            for a in range(SIGNALS):
                for part in range(2):
                    high, low = split(products[a][part])
                    product_ref[0, j, a, rows, lanes(part)] = high
                    product_ref[1, j, a, rows, lanes(part)] = low
        for a in range(SIGNALS):
            high, low = product_ref[0, j, a], product_ref[1, j, a]
            u_ref[j, a] = (
                dot(high, last_back_ref[0, j])
                + dot(low, last_back_ref[0, j])
                + dot(high, last_back_ref[1, j])
            )

    for a in range(SIGNALS):
        for rows in chunks:
            imag_rows = slice(ROWS + rows.start, ROWS + rows.stop)
            z = [(u_ref[j, a, rows, lanes(0)], u_ref[j, a, rows, lanes(1)]) for j in range(TURNS)]
            z = four_point(z, 1)
            for p in range(TURNS):
                cos, sin = turn_ref[0, rows, lanes(p)], turn_ref[1, rows, lanes(p)]
                real, imag = times(z[p], cos, sin)
                for part, place in ((real, rows), (imag, imag_rows)):
                    high, low = split(part)
                    v_ref[0, a, place, lanes(p)] = high
                    v_ref[1, a, place, lanes(p)] = low
        for pair in range(TURNS // 2):
            columns = slice(2 * pair * INNER, 2 * (pair + 1) * INNER)
            high, low = v_ref[0, a, :, columns], v_ref[1, a, :, columns]
            out = (
                dot(first_back_ref[0], high)
                + dot(first_back_ref[0], low)
                + dot(first_back_ref[1], high)
            )
            for p in range(2):
                y_ref[:, a, 2 * pair + p] = out[:, lanes(p)].reshape(blocks, block_rows, INNER)


def in_vmem(count):
    return [pl.BlockSpec(memory_space=pltpu.VMEM)] * count


def convolve(received, scale):
    constants = [jnp.asarray(table) for table in tables(scale)]
    width = TURNS * INNER
    return pl.pallas_call(
        convolve_kernel,
        out_shape=jax.ShapeDtypeStruct(received.shape, F32),
        in_specs=in_vmem(6),
        out_specs=pl.BlockSpec(memory_space=pltpu.VMEM),
        scratch_shapes=[
            pltpu.VMEM((SIGNALS, 2 * ROWS, width), F32),
            pltpu.VMEM((2, TURNS, SIGNALS, ROWS, 2 * INNER), BF16),
            pltpu.VMEM((TURNS, SIGNALS, ROWS, 2 * INNER), F32),
            pltpu.VMEM((2, TURNS, SIGNALS, ROWS, 2 * INNER), BF16),
            pltpu.VMEM((TURNS, SIGNALS, ROWS, 2 * INNER), F32),
            pltpu.VMEM((2, SIGNALS, 2 * ROWS, width), BF16),
        ],
        compiler_params=pltpu.CompilerParams(vmem_limit_bytes=VMEM_BYTES),
        name="convolve",
    )(received, *constants)


def grid_points(block_rows):
    for m in range(block_rows):
        for p in range(TURNS):
            yield lanes(m * TURNS + p), p * block_rows + m


def pack_kernel(block_rows, place_ref, q_ref, k_ref, v_ref, o_ref, f_ref, sent_ref):
    chan = place_ref[0]
    signal = TURNS * block_rows
    stride = SIGNALS * signal
    for tile in range(0, q_ref.shape[0], 2 * GROUP):
        rows = slice(tile, tile + 2 * GROUP)
        bases = [
            jnp.bitwise_xor(chan, (tile + h * GROUP) // GROUP) * (GROUP * stride) for h in range(2)
        ]
        for columns, row in grid_points(block_rows):
            values = (
                k_ref[rows, columns].astype(F32) * v_ref[rows, columns].astype(F32),
                q_ref[rows, columns].astype(F32) * o_ref[rows, columns].astype(F32),
                f_ref[rows, columns],
            )
            for h in range(2):
                for a in range(SIGNALS):
                    sent_ref[pl.ds(bases[h] + a * signal + row, GROUP, stride=stride), :] = values[
                        a
                    ][h * GROUP : (h + 1) * GROUP]


def unpack_kernel(block_rows, place_ref, back_ref, k_ref, v_ref, o_ref, qg_ref, kg_ref, vg_ref):
    chan = place_ref[0]
    signal = TURNS * block_rows
    stride = SIGNALS * signal
    for tile in range(0, k_ref.shape[0], 2 * GROUP):
        rows = slice(tile, tile + 2 * GROUP)
        bases = [
            jnp.bitwise_xor(chan, (tile + h * GROUP) // GROUP) * (GROUP * stride) for h in range(2)
        ]
        for columns, row in grid_points(block_rows):
            conv_out, adjoint = [
                jnp.concatenate(
                    [
                        back_ref[pl.ds(bases[h] + a * signal + row, GROUP, stride=stride), :]
                        for h in range(2)
                    ],
                    axis=0,
                )
                for a in range(2)
            ]
            qg_ref[rows, columns] = (conv_out * o_ref[rows, columns].astype(F32)).astype(BF16)
            kg_ref[rows, columns] = (adjoint * v_ref[rows, columns].astype(F32)).astype(BF16)
            vg_ref[rows, columns] = (adjoint * k_ref[rows, columns].astype(F32)).astype(BF16)


def total_kernel(block_rows, *refs):
    grad_ref = refs[-1]
    signal = TURNS * block_rows
    for columns, row in grid_points(block_rows):
        values = [ref[pl.ds(row, GROUP, stride=signal), :] for ref in refs[:-1]]
        total = values[0]
        for value in values[1:]:
            total = total + value
        grad_ref[:, columns] = total


def local_call(kernel, name, out_shape, place, *arrays):
    count = len(arrays)
    specs = in_vmem(count)
    if place is not None:
        specs = [pl.BlockSpec(memory_space=pltpu.SMEM)] + specs
        arrays = (place,) + arrays
    single = not isinstance(out_shape, tuple)
    return pl.pallas_call(
        kernel,
        out_shape=out_shape,
        in_specs=specs,
        out_specs=in_vmem(1)[0] if single else tuple(in_vmem(len(out_shape))),
        compiler_params=pltpu.CompilerParams(vmem_limit_bytes=VMEM_BYTES),
        name=name,
    )(*arrays)


def shards(query_proj, key_proj, value_proj, out_cotangent, filter_raw):
    slab, width = query_proj.shape
    parts = lax.axis_size("seq")
    groups = lax.axis_size("chan")
    length = parts * width
    scale = 1.0 / (length * math.sqrt(length))
    block_rows = ROWS // parts
    place = lax.axis_index("chan").astype(jnp.int32).reshape(1)
    flat = (slab * SIGNALS * TURNS * block_rows, INNER)
    sent = local_call(
        functools.partial(pack_kernel, block_rows),
        "pack",
        jax.ShapeDtypeStruct(flat, F32),
        place,
        query_proj,
        key_proj,
        value_proj,
        out_cotangent,
        filter_raw,
    )
    sent = sent.reshape(slab, SIGNALS, TURNS, block_rows, INNER)
    received = lax.all_to_all(sent, "seq", split_axis=0, concat_axis=0, tiled=True)
    signals = convolve(received, scale)
    back = lax.all_to_all(signals, "seq", split_axis=0, concat_axis=0, tiled=True)
    pieces = []
    for k in range(groups):
        piece = back[k * GROUP : (k + 1) * GROUP, 2]
        if k > 0:
            piece = lax.ppermute(piece, "chan", [(c, c ^ k) for c in range(groups)])
        pieces.append(piece.reshape(-1, INNER))
    grads = local_call(
        functools.partial(unpack_kernel, block_rows),
        "unpack",
        (jax.ShapeDtypeStruct((slab, width), BF16),) * 3,
        place,
        back.reshape(flat),
        key_proj,
        value_proj,
        out_cotangent,
    )
    filter_grad = local_call(
        functools.partial(total_kernel, block_rows),
        "total",
        jax.ShapeDtypeStruct((slab // groups, width), F32),
        None,
        *pieces,
    )
    return (*grads, filter_grad)


def solution(mesh):
    placed = (
        P("chan", "seq"),
        P("chan", "seq"),
        P("chan", "seq"),
        P("chan", "seq"),
        P(None, "seq"),
    )
    return jax.shard_map(
        shards,
        mesh=mesh,
        in_specs=placed,
        out_specs=(P("chan", "seq"), P("chan", "seq"), P("chan", "seq"), P("chan", "seq")),
        check_vma=False,
    )
```

```python
import functools
import itertools
import math

import jax
import jax.numpy as jnp
import ml_dtypes
import numpy as np
from jax import lax
from jax.experimental import pallas as pl
from jax.experimental.pallas import tpu as pltpu
from jax.sharding import PartitionSpec as P

F32 = jnp.float32
BF16 = jnp.bfloat16
SIGNALS = 3
ROWS = 256
TURNS = 4
INNER = 128
CHUNK = 16
GROUP = 8
VMEM_BYTES = 28 * 1024 * 1024
PACK_BYTES = 58 * 1024 * 1024


def halves(table):
    table = table.astype(np.float32)
    high = table.astype(ml_dtypes.bfloat16)
    low = (table - high.astype(np.float32)).astype(ml_dtypes.bfloat16)
    return np.stack([high, low])


def tables(scale):
    width = TURNS * INNER
    k = np.arange(ROWS)[:, None] + 0.25
    angle = 2.0 * np.pi * k * np.arange(ROWS)[None, :] / ROWS
    first = np.concatenate([np.cos(angle), -np.sin(angle)], axis=0)
    turn = 2.0 * np.pi * k * np.arange(width)[None, :] / (ROWS * width)
    turn = np.stack([np.cos(turn), np.sin(turn)]).astype(np.float32)
    l = np.arange(INNER)
    lasts = []
    for j in range(TURNS):
        angle = 2.0 * np.pi * (l[:, None] * (j + TURNS * l[None, :]) % width) / width
        cos, sin = np.cos(angle), np.sin(angle)
        lasts.append(
            np.concatenate(
                [np.concatenate([cos, -sin], axis=1), np.concatenate([sin, cos], axis=1)], axis=0
            )
        )
    last = np.stack(lasts)
    return (
        halves(first),
        halves(first.T),
        turn,
        halves(last),
        halves(last.transpose(0, 2, 1) * scale),
    )


def times(pair, cos, sin):
    return pair[0] * cos - pair[1] * sin, pair[1] * cos + pair[0] * sin


def add(first, second):
    return first[0] + second[0], first[1] + second[1]


def sub(first, second):
    return first[0] - second[0], first[1] - second[1]


def quarter(pair, sign):
    return (-pair[1], pair[0]) if sign > 0 else (pair[1], -pair[0])


def four_point(z, sign):
    s0, d0 = add(z[0], z[2]), sub(z[0], z[2])
    s1, d1 = add(z[1], z[3]), sub(z[1], z[3])
    if sign > 0:
        return [
            add(s0, s1),
            (d0[0] - d1[1], d0[1] + d1[0]),
            sub(s0, s1),
            (d0[0] + d1[1], d0[1] - d1[0]),
        ]
    return [
        add(s0, s1),
        (d0[0] + d1[1], d0[1] - d1[0]),
        sub(s0, s1),
        (d0[0] - d1[1], d0[1] + d1[0]),
    ]


def split(value):
    high = value.astype(BF16)
    return high, (value - high.astype(F32)).astype(BF16)


def dot(first, second):
    return jnp.dot(first, second, preferred_element_type=F32)


def lanes(index):
    return slice(index * INNER, (index + 1) * INNER)


def convolve_kernel(
    x_ref,
    first_ref,
    first_back_ref,
    turn_ref,
    last_ref,
    last_back_ref,
    y_ref,
    mixed_ref,
    z_ref,
    spectra_ref,
    product_ref,
    u_ref,
    v_ref,
):
    blocks, _, _, block_rows, _ = x_ref.shape
    half = ROWS
    chunks = [slice(i, i + CHUNK) for i in range(0, ROWS, CHUNK)]

    def imag(rows):
        return slice(ROWS + rows.start, ROWS + rows.stop)

    def columns(pair):
        return slice(2 * pair * INNER, 2 * (pair + 1) * INNER)

    def mix(a, pair, part):
        data = jnp.concatenate(
            [x_ref[:, a, 2 * pair + p].reshape(ROWS, INNER) for p in range(2)], axis=1
        )
        high, low = split(data)
        rows = slice(part * half, (part + 1) * half)
        mixed_ref[a, rows, columns(pair)] = (
            dot(first_ref[0, rows], high)
            + dot(first_ref[0, rows], low)
            + dot(first_ref[1, rows], high)
        )

    def opening(a, rows):
        z = []
        for p in range(TURNS):
            cos, sin = turn_ref[0, rows, lanes(p)], turn_ref[1, rows, lanes(p)]
            pair = (mixed_ref[a, rows, lanes(p)], mixed_ref[a, imag(rows), lanes(p)])
            z.append(times(pair, cos, -sin))
        z = four_point(z, -1)
        for j in range(TURNS):
            for part in range(2):
                high, low = split(z[j][part])
                z_ref[0, j, a, rows, lanes(part)] = high
                z_ref[1, j, a, rows, lanes(part)] = low

    def last(j, a):
        high, low = z_ref[0, j, a], z_ref[1, j, a]
        spectra_ref[j, a] = (
            dot(high, last_ref[0, j]) + dot(low, last_ref[0, j]) + dot(high, last_ref[1, j])
        )

    def product(j, rows):
        gated, carried, filters = [
            (spectra_ref[j, a, rows, lanes(0)], spectra_ref[j, a, rows, lanes(1)])
            for a in range(SIGNALS)
        ]
        products = (
            times(gated, filters[0], filters[1]),
            times(carried, filters[0], -filters[1]),
            times(carried, gated[0], -gated[1]),
        )
        for a in range(SIGNALS):
            for part in range(2):
                high, low = split(products[a][part])
                product_ref[0, j, a, rows, lanes(part)] = high
                product_ref[1, j, a, rows, lanes(part)] = low

    def last_back(j, a):
        high, low = product_ref[0, j, a], product_ref[1, j, a]
        u_ref[j, a] = (
            dot(high, last_back_ref[0, j])
            + dot(low, last_back_ref[0, j])
            + dot(high, last_back_ref[1, j])
        )

    def closing(a, rows):
        z = [(u_ref[j, a, rows, lanes(0)], u_ref[j, a, rows, lanes(1)]) for j in range(TURNS)]
        z = four_point(z, 1)
        for p in range(TURNS):
            cos, sin = turn_ref[0, rows, lanes(p)], turn_ref[1, rows, lanes(p)]
            pair = times(z[p], cos, sin)
            for part, place in zip(pair, (rows, imag(rows))):
                high, low = split(part)
                v_ref[0, a, place, lanes(p)] = high
                v_ref[1, a, place, lanes(p)] = low

    def unmix(a, pair):
        high, low = v_ref[0, a, :, columns(pair)], v_ref[1, a, :, columns(pair)]
        out = (
            dot(first_back_ref[0], high)
            + dot(first_back_ref[0], low)
            + dot(first_back_ref[1], high)
        )
        for p in range(2):
            y_ref[:, a, 2 * pair + p] = out[:, lanes(p)].reshape(blocks, block_rows, INNER)

    def steps(function, *ranges):
        return [functools.partial(function, *place) for place in itertools.product(*ranges)]

    pairs, turns = range(TURNS // 2), range(TURNS)
    for matrix, vector in (
        (steps(mix, [2], pairs, range(2)), []),
        (steps(mix, [0], pairs, range(2)), steps(opening, [2], chunks)),
        (steps(mix, [1], pairs, range(2)), steps(opening, [0], chunks)),
        (steps(last, turns, [2, 0]), steps(opening, [1], chunks)),
        (steps(last, [0], [1]), []),
        (steps(last, turns[1:], [1]), steps(product, [0], chunks)),
        (steps(last_back, [0], range(SIGNALS)), steps(product, [1], chunks)),
        (steps(last_back, [1], range(SIGNALS)), steps(product, [2], chunks)),
        (steps(last_back, [2], range(SIGNALS)), steps(product, [3], chunks)),
        (steps(last_back, [3], [0]), []),
        (steps(last_back, [3], [1, 2]), steps(closing, [0], chunks)),
        (steps(unmix, [0], pairs), steps(closing, [1], chunks)),
        (steps(unmix, [1], pairs), steps(closing, [2], chunks)),
        (steps(unmix, [2], pairs), []),
    ):
        for i, step in enumerate(matrix):
            step()
            for other in vector[i * len(vector) // len(matrix) : (i + 1) * len(vector) // len(matrix)]:
                other()


def in_vmem(count):
    return [pl.BlockSpec(memory_space=pltpu.VMEM)] * count


def convolve(received, scale):
    constants = [jnp.asarray(table) for table in tables(scale)]
    width = TURNS * INNER
    return pl.pallas_call(
        convolve_kernel,
        out_shape=jax.ShapeDtypeStruct(received.shape, F32),
        in_specs=in_vmem(6),
        out_specs=pl.BlockSpec(memory_space=pltpu.VMEM),
        scratch_shapes=[
            pltpu.VMEM((SIGNALS, 2 * ROWS, width), F32),
            pltpu.VMEM((2, TURNS, SIGNALS, ROWS, 2 * INNER), BF16),
            pltpu.VMEM((TURNS, SIGNALS, ROWS, 2 * INNER), F32),
            pltpu.VMEM((2, TURNS, SIGNALS, ROWS, 2 * INNER), BF16),
            pltpu.VMEM((TURNS, SIGNALS, ROWS, 2 * INNER), F32),
            pltpu.VMEM((2, SIGNALS, 2 * ROWS, width), BF16),
        ],
        compiler_params=pltpu.CompilerParams(vmem_limit_bytes=VMEM_BYTES),
        name="convolve",
    )(received, *constants)


def pack_kernel(block_rows, place_ref, *refs):
    sources, sent_ref, held, sems = refs[:5], refs[5], refs[6:11], refs[11]
    chan = place_ref[0]
    signal = TURNS * block_rows
    stride = SIGNALS * signal
    tall = 2 * GROUP
    tiles = range(0, sources[0].shape[0], tall)
    copies = []
    for t, tile in enumerate(tiles):
        for n in range(5):
            rows = pl.ds(tile, tall)
            copies.append(pltpu.make_async_copy(sources[n].at[rows], held[n].at[rows], sems.at[t, n]))
    for copy in copies:
        copy.start()
    q_ref, k_ref, v_ref, o_ref, f_ref = held
    for t, tile in enumerate(tiles):
        for copy in copies[5 * t : 5 * t + 5]:
            copy.wait()
        rows = slice(tile, tile + tall)
        bases = [jnp.bitwise_xor(chan, (tile + h * GROUP) // GROUP) * GROUP for h in range(2)]
        for p in range(TURNS):
            values = [[], [], []]
            for m in range(block_rows):
                columns = lanes(m * TURNS + p)
                values[0].append(k_ref[rows, columns].astype(F32) * v_ref[rows, columns].astype(F32))
                values[1].append(q_ref[rows, columns].astype(F32) * o_ref[rows, columns].astype(F32))
                values[2].append(f_ref[rows, columns])
            for h in range(2):
                for a in range(SIGNALS):
                    block = jnp.stack([value[h * GROUP : (h + 1) * GROUP] for value in values[a]])
                    sent_ref[pl.ds(bases[h], GROUP), a, p] = jnp.swapaxes(block, 0, 1)


def unpack_kernel(block_rows, place_ref, back_ref, k_ref, v_ref, o_ref, qg_ref, kg_ref, vg_ref):
    chan = place_ref[0]
    tall = 2 * GROUP
    for tile in range(0, k_ref.shape[0], tall):
        rows = slice(tile, tile + tall)
        bases = [jnp.bitwise_xor(chan, (tile + h * GROUP) // GROUP) * GROUP for h in range(2)]
        for p in range(TURNS):
            conv_out, adjoint = [
                jnp.concatenate(
                    [
                        jnp.swapaxes(back_ref[pl.ds(bases[h], GROUP), a, p], 0, 1)
                        for h in range(2)
                    ],
                    axis=1,
                )
                for a in range(2)
            ]
            for m in range(block_rows):
                columns = lanes(m * TURNS + p)
                qg_ref[rows, columns] = (conv_out[m] * o_ref[rows, columns].astype(F32)).astype(BF16)
                kg_ref[rows, columns] = (adjoint[m] * v_ref[rows, columns].astype(F32)).astype(BF16)
                vg_ref[rows, columns] = (adjoint[m] * k_ref[rows, columns].astype(F32)).astype(BF16)


def total_kernel(block_rows, *refs):
    grad_ref = refs[-1]
    for p in range(TURNS):
        total = refs[0][:, p]
        for ref in refs[1:-1]:
            total = total + ref[:, p]
        total = jnp.swapaxes(total, 0, 1)
        for m in range(block_rows):
            grad_ref[:, lanes(m * TURNS + p)] = total[m]


def local_call(kernel, name, out_shape, place, *arrays):
    count = len(arrays)
    specs = in_vmem(count)
    if place is not None:
        specs = [pl.BlockSpec(memory_space=pltpu.SMEM)] + specs
        arrays = (place,) + arrays
    single = not isinstance(out_shape, tuple)
    return pl.pallas_call(
        kernel,
        out_shape=out_shape,
        in_specs=specs,
        out_specs=in_vmem(1)[0] if single else tuple(in_vmem(len(out_shape))),
        compiler_params=pltpu.CompilerParams(vmem_limit_bytes=VMEM_BYTES),
        name=name,
    )(*arrays)


def pack(block_rows, place, arrays):
    slab, width = arrays[0].shape
    shape = (slab, SIGNALS, TURNS, block_rows, INNER)
    return pl.pallas_call(
        functools.partial(pack_kernel, block_rows),
        out_shape=jax.ShapeDtypeStruct(shape, F32),
        in_specs=[pl.BlockSpec(memory_space=pltpu.SMEM)] + [pl.BlockSpec(memory_space=pl.ANY)] * 5,
        out_specs=pl.BlockSpec(memory_space=pltpu.VMEM),
        scratch_shapes=[pltpu.VMEM((slab, width), array.dtype) for array in arrays]
        + [pltpu.SemaphoreType.DMA((slab // (2 * GROUP), 5))],
        compiler_params=pltpu.CompilerParams(vmem_limit_bytes=PACK_BYTES),
        name="pack",
    )(place, *arrays)


def shards(query_proj, key_proj, value_proj, out_cotangent, filter_raw):
    slab, width = query_proj.shape
    parts = lax.axis_size("seq")
    groups = lax.axis_size("chan")
    length = parts * width
    scale = 1.0 / (length * math.sqrt(length))
    block_rows = ROWS // parts
    place = lax.axis_index("chan").astype(jnp.int32).reshape(1)
    sent = pack(
        block_rows, place, (query_proj, key_proj, value_proj, out_cotangent, filter_raw)
    )
    received = lax.all_to_all(sent, "seq", split_axis=0, concat_axis=0, tiled=True)
    signals = convolve(received, scale)
    back = lax.all_to_all(signals, "seq", split_axis=0, concat_axis=0, tiled=True)
    pieces = []
    for k in range(groups):
        piece = back[k * GROUP : (k + 1) * GROUP, 2]
        if k > 0:
            piece = lax.ppermute(piece, "chan", [(c, c ^ k) for c in range(groups)])
        pieces.append(piece)
    grads = local_call(
        functools.partial(unpack_kernel, block_rows),
        "unpack",
        (jax.ShapeDtypeStruct((slab, width), BF16),) * 3,
        place,
        back,
        key_proj,
        value_proj,
        out_cotangent,
    )
    filter_grad = local_call(
        functools.partial(total_kernel, block_rows),
        "total",
        jax.ShapeDtypeStruct((slab // groups, width), F32),
        None,
        *pieces,
    )
    return (*grads, filter_grad)


def solution(mesh):
    placed = (
        P("chan", "seq"),
        P("chan", "seq"),
        P("chan", "seq"),
        P("chan", "seq"),
        P(None, "seq"),
    )
    return jax.shard_map(
        shards,
        mesh=mesh,
        in_specs=placed,
        out_specs=(P("chan", "seq"), P("chan", "seq"), P("chan", "seq"), P("chan", "seq")),
        check_vma=False,
    )
```

```python
import functools
import itertools
import math

import jax
import jax.numpy as jnp
import ml_dtypes
import numpy as np
from jax import lax
from jax.experimental import pallas as pl
from jax.experimental.pallas import tpu as pltpu
from jax.sharding import PartitionSpec as P

F32 = jnp.float32
BF16 = jnp.bfloat16
SIGNALS = 3
ROWS = 256
TURNS = 4
INNER = 128
CHUNK = 16
GROUP = 8
VMEM_BYTES = 28 * 1024 * 1024
PACK_BYTES = 58 * 1024 * 1024


def halves(table):
    table = table.astype(np.float32)
    high = table.astype(ml_dtypes.bfloat16)
    low = (table - high.astype(np.float32)).astype(ml_dtypes.bfloat16)
    return np.stack([high, low])


def tables(scale):
    width = TURNS * INNER
    k = np.arange(ROWS)[:, None] + 0.25
    angle = 2.0 * np.pi * k * np.arange(ROWS)[None, :] / ROWS
    first = np.concatenate([np.cos(angle), -np.sin(angle)], axis=0)
    turn = 2.0 * np.pi * k * np.arange(width)[None, :] / (ROWS * width)
    turn = np.stack([np.cos(turn), np.sin(turn)]).astype(np.float32)
    l = np.arange(INNER)
    lasts = []
    for j in range(TURNS):
        angle = 2.0 * np.pi * (l[:, None] * (j + TURNS * l[None, :]) % width) / width
        cos, sin = np.cos(angle), np.sin(angle)
        lasts.append(
            np.concatenate(
                [np.concatenate([cos, -sin], axis=1), np.concatenate([sin, cos], axis=1)], axis=0
            )
        )
    last = np.stack(lasts)
    return (
        halves(first),
        halves(first.T),
        turn,
        halves(last),
        halves(last.transpose(0, 2, 1) * scale),
    )


def times(pair, cos, sin):
    return pair[0] * cos - pair[1] * sin, pair[1] * cos + pair[0] * sin


def add(first, second):
    return first[0] + second[0], first[1] + second[1]


def sub(first, second):
    return first[0] - second[0], first[1] - second[1]


def quarter(pair, sign):
    return (-pair[1], pair[0]) if sign > 0 else (pair[1], -pair[0])


def four_point(z, sign):
    s0, d0 = add(z[0], z[2]), sub(z[0], z[2])
    s1, d1 = add(z[1], z[3]), sub(z[1], z[3])
    if sign > 0:
        return [
            add(s0, s1),
            (d0[0] - d1[1], d0[1] + d1[0]),
            sub(s0, s1),
            (d0[0] + d1[1], d0[1] - d1[0]),
        ]
    return [
        add(s0, s1),
        (d0[0] + d1[1], d0[1] - d1[0]),
        sub(s0, s1),
        (d0[0] - d1[1], d0[1] + d1[0]),
    ]


def split(value):
    high = value.astype(BF16)
    return high, (value - high.astype(F32)).astype(BF16)


def dot(first, second):
    return jnp.dot(first, second, preferred_element_type=F32)


def lanes(index):
    return slice(index * INNER, (index + 1) * INNER)


def imag(rows):
    return slice(ROWS + rows.start, ROWS + rows.stop)


def columns(pair):
    return slice(2 * pair * INNER, 2 * (pair + 1) * INNER)


def mix(x_ref, first_ref, mixed_ref, a, pair, part):
    data = jnp.concatenate(
        [x_ref[:, a, 2 * pair + p].reshape(ROWS, INNER) for p in range(2)], axis=1
    )
    high, low = split(data)
    rows = slice(part * ROWS, (part + 1) * ROWS)
    mixed_ref[rows, columns(pair)] = (
        dot(first_ref[0, rows], high)
        + dot(first_ref[0, rows], low)
        + dot(first_ref[1, rows], high)
    )


def opening(mixed_ref, turn_ref, z_ref, rows):
    z = []
    for p in range(TURNS):
        cos, sin = turn_ref[0, rows, lanes(p)], turn_ref[1, rows, lanes(p)]
        pair = (mixed_ref[rows, lanes(p)], mixed_ref[imag(rows), lanes(p)])
        z.append(times(pair, cos, -sin))
    z = four_point(z, -1)
    for j in range(TURNS):
        for part in range(2):
            high, low = split(z[j][part])
            z_ref[0, j, rows, lanes(part)] = high
            z_ref[1, j, rows, lanes(part)] = low


def last(z_ref, last_ref, spectra_ref, j):
    high, low = z_ref[0, j], z_ref[1, j]
    spectra_ref[j] = (
        dot(high, last_ref[0, j]) + dot(low, last_ref[0, j]) + dot(high, last_ref[1, j])
    )


def product(one_ref, two_ref, conjugate, product_ref, j, rows):
    one = (one_ref[j, rows, lanes(0)], one_ref[j, rows, lanes(1)])
    two = (two_ref[j, rows, lanes(0)], two_ref[j, rows, lanes(1)])
    pair = times(one, two[0], -two[1] if conjugate else two[1])
    for part in range(2):
        high, low = split(pair[part])
        product_ref[0, j, rows, lanes(part)] = high
        product_ref[1, j, rows, lanes(part)] = low


def closing(u_ref, turn_ref, v_ref, rows):
    z = [(u_ref[j, rows, lanes(0)], u_ref[j, rows, lanes(1)]) for j in range(TURNS)]
    z = four_point(z, 1)
    for p in range(TURNS):
        cos, sin = turn_ref[0, rows, lanes(p)], turn_ref[1, rows, lanes(p)]
        pair = times(z[p], cos, sin)
        for part, place in zip(pair, (rows, imag(rows))):
            high, low = split(part)
            v_ref[0, place, lanes(p)] = high
            v_ref[1, place, lanes(p)] = low


def unmix(v_ref, first_back_ref, store, pair):
    high, low = v_ref[0, :, columns(pair)], v_ref[1, :, columns(pair)]
    out = (
        dot(first_back_ref[0], high)
        + dot(first_back_ref[0], low)
        + dot(first_back_ref[1], high)
    )
    for p in range(2):
        store(2 * pair + p, out[:, lanes(p)])


def steps(function, *ranges):
    return [functools.partial(function, *place) for place in itertools.product(*ranges)]


def interleave(*lines):
    for matrix, vector in lines:
        count = max(len(matrix), 1)
        for i in range(count):
            for step in matrix[i : i + 1]:
                step()
            for step in vector[i * len(vector) // count : (i + 1) * len(vector) // count]:
                step()


CHUNKS = [slice(i, i + CHUNK) for i in range(0, ROWS, CHUNK)]
PAIRS = range(TURNS // 2)
ALL_TURNS = range(TURNS)


def correlate_kernel(
    core_ref,
    x_ref,
    first_ref,
    first_back_ref,
    turn_ref,
    last_ref,
    last_back_ref,
    gated_ref,
    carried_ref,
    kept_ref,
    given_ref,
    mixed_ref,
    z_ref,
    product_ref,
    u_ref,
    v_ref,
    halves_ref,
):
    blocks, _, _, block_rows, _ = x_ref.shape
    core = core_ref[0]

    def store(p, value):
        halves_ref[p // 2, :, p % 2] = value.reshape(blocks, block_rows, INNER)

    spectra = (gated_ref, carried_ref)
    mixes = [functools.partial(mix, x_ref, first_ref, mixed_ref.at[a], a) for a in range(2)]
    opens = [functools.partial(opening, mixed_ref.at[a], turn_ref, z_ref.at[a]) for a in range(2)]
    lasts = [functools.partial(last, z_ref.at[a], last_ref, spectra[a]) for a in range(2)]
    products = functools.partial(product, carried_ref, gated_ref, True, product_ref)
    last_back = functools.partial(last, product_ref, last_back_ref, u_ref)
    close = functools.partial(closing, u_ref, turn_ref, v_ref)
    interleave(
        (steps(mixes[0], PAIRS, range(2)), []),
        (steps(mixes[1], PAIRS, range(2)), steps(opens[0], CHUNKS)),
        (steps(lasts[0], ALL_TURNS), steps(opens[1], CHUNKS)),
        (steps(lasts[1], [0]), []),
        (steps(lasts[1], ALL_TURNS[1:]), steps(products, ALL_TURNS[:-1], CHUNKS)),
        (steps(last_back, ALL_TURNS[:-1]), steps(products, ALL_TURNS[-1:], CHUNKS)),
        (steps(last_back, ALL_TURNS[-1:]), []),
        ([], steps(close, CHUNKS)),
        (steps(functools.partial(unmix, v_ref, first_back_ref, store), PAIRS), []),
    )
    kept_ref[...] = halves_ref[core]
    given_ref[...] = halves_ref[1 - core]


def convolve_kernel(
    x_ref,
    gated_ref,
    carried_ref,
    first_ref,
    first_back_ref,
    turn_ref,
    last_ref,
    last_back_ref,
    conv_ref,
    v_ref,
    mixed_ref,
    z_ref,
    filter_ref,
    product_ref,
    u_ref,
    v_conv_ref,
):
    blocks, _, _, block_rows, _ = x_ref.shape

    def store(p, value):
        conv_ref[:, p] = value.reshape(blocks, block_rows, INNER)

    v_refs = (v_conv_ref, v_ref)
    mixes = functools.partial(mix, x_ref, first_ref, mixed_ref, 2)
    opens = functools.partial(opening, mixed_ref, turn_ref, z_ref)
    lasts = functools.partial(last, z_ref, last_ref, filter_ref)

    def products(j, rows):
        product(gated_ref, filter_ref, False, product_ref.at[0], j, rows)
        product(carried_ref, filter_ref, True, product_ref.at[1], j, rows)

    def last_back(j, a):
        last(product_ref.at[a], last_back_ref, u_ref.at[a], j)

    close = [
        functools.partial(closing, u_ref.at[a], turn_ref, v_refs[a]) for a in range(2)
    ]
    interleave(
        (steps(mixes, PAIRS, range(2)), []),
        ([], steps(opens, CHUNKS)),
        (steps(lasts, [0]), []),
        (steps(lasts, ALL_TURNS[1:]), steps(products, ALL_TURNS[:-1], CHUNKS)),
        (steps(last_back, ALL_TURNS[:-1], range(2)), steps(products, ALL_TURNS[-1:], CHUNKS)),
        (steps(last_back, ALL_TURNS[-1:], [0]), []),
        (steps(last_back, ALL_TURNS[-1:], [1]), steps(close[0], CHUNKS)),
        (
            steps(functools.partial(unmix, v_conv_ref, first_back_ref, store), PAIRS),
            steps(close[1], CHUNKS),
        ),
    )


def gather_kernel(conv_ref, v_ref, first_back_ref, kept_ref, taken_ref, out_ref):
    blocks, _, block_rows, _ = conv_ref.shape

    def store(p, value):
        out_ref[:, TURNS + p] = value.reshape(blocks, block_rows, INNER)

    def rest(p):
        out_ref[:, p] = conv_ref[:, p]
        if p < 2:
            out_ref[:, 2 * TURNS + p] = kept_ref[:, p] + taken_ref[:, p]

    interleave(
        (steps(functools.partial(unmix, v_ref, first_back_ref, store), PAIRS), steps(rest, ALL_TURNS))
    )


def in_vmem(count):
    return [pl.BlockSpec(memory_space=pltpu.VMEM)] * count


def convolve(core, received, scale, exchange):
    first, first_back, turn, last_table, last_back = [
        jnp.asarray(table) for table in tables(scale)
    ]
    width = TURNS * INNER
    blocks, _, _, block_rows, _ = received.shape
    spectrum = (TURNS, ROWS, 2 * INNER)
    two_halves = jax.ShapeDtypeStruct((blocks, 2, block_rows, INNER), F32)
    params = pltpu.CompilerParams(vmem_limit_bytes=VMEM_BYTES)
    gated, carried, kept, given = pl.pallas_call(
        correlate_kernel,
        out_shape=(jax.ShapeDtypeStruct(spectrum, F32),) * 2 + (two_halves,) * 2,
        in_specs=[pl.BlockSpec(memory_space=pltpu.SMEM)] + in_vmem(6),
        out_specs=tuple(in_vmem(4)),
        scratch_shapes=[
            pltpu.VMEM((2, 2 * ROWS, width), F32),
            pltpu.VMEM((2, 2, *spectrum), BF16),
            pltpu.VMEM((2, *spectrum), BF16),
            pltpu.VMEM(spectrum, F32),
            pltpu.VMEM((2, 2 * ROWS, width), BF16),
            pltpu.VMEM((2, *two_halves.shape), F32),
        ],
        compiler_params=params,
        name="correlate",
    )(core, received, first, first_back, turn, last_table, last_back)
    taken = exchange(given)
    conv_out, mixed_adjoint = pl.pallas_call(
        convolve_kernel,
        out_shape=(
            jax.ShapeDtypeStruct((blocks, TURNS, block_rows, INNER), F32),
            jax.ShapeDtypeStruct((2, 2 * ROWS, width), BF16),
        ),
        in_specs=in_vmem(8),
        out_specs=tuple(in_vmem(2)),
        scratch_shapes=[
            pltpu.VMEM((2 * ROWS, width), F32),
            pltpu.VMEM((2, *spectrum), BF16),
            pltpu.VMEM(spectrum, F32),
            pltpu.VMEM((2, 2, *spectrum), BF16),
            pltpu.VMEM((2, *spectrum), F32),
            pltpu.VMEM((2, 2 * ROWS, width), BF16),
        ],
        compiler_params=params,
        name="convolve",
    )(received, gated, carried, first, first_back, turn, last_table, last_back)
    return pl.pallas_call(
        gather_kernel,
        out_shape=jax.ShapeDtypeStruct((blocks, 2 * TURNS + 2, block_rows, INNER), F32),
        in_specs=in_vmem(5),
        out_specs=in_vmem(1)[0],
        compiler_params=params,
        name="gather",
    )(conv_out, mixed_adjoint, first_back, kept, taken)


def pack_kernel(block_rows, place_ref, *refs):
    sources, sent_ref, held, built, sems, out_sems = refs[:5], refs[5], refs[6:11], *refs[11:]
    chan = place_ref[0]
    tall = 2 * GROUP
    tiles = range(0, sources[0].shape[0], tall)
    copies = []
    for t, tile in enumerate(tiles):
        for n in range(5):
            rows = pl.ds(tile, tall)
            copies.append(pltpu.make_async_copy(sources[n].at[rows], held[n].at[rows], sems.at[t, n]))
    for copy in copies:
        copy.start()
    outgoing = []
    q_ref, k_ref, v_ref, o_ref, f_ref = held
    for t, tile in enumerate(tiles):
        for copy in copies[5 * t : 5 * t + 5]:
            copy.wait()
        rows = slice(tile, tile + tall)
        for p in range(TURNS):
            values = [[], [], []]
            for m in range(block_rows):
                columns = lanes(m * TURNS + p)
                values[0].append(k_ref[rows, columns].astype(F32) * v_ref[rows, columns].astype(F32))
                values[1].append(q_ref[rows, columns].astype(F32) * o_ref[rows, columns].astype(F32))
                values[2].append(f_ref[rows, columns])
            for h in range(2):
                for a in range(SIGNALS):
                    block = jnp.stack([value[h * GROUP : (h + 1) * GROUP] for value in values[a]])
                    start = tile + h * GROUP
                    built[start : start + GROUP, a, p] = jnp.swapaxes(block, 0, 1)
        for h in range(2):
            start = tile + h * GROUP
            target = jnp.bitwise_xor(chan, start // GROUP) * GROUP
            copy = pltpu.make_async_copy(
                built.at[pl.ds(start, GROUP)], sent_ref.at[pl.ds(target, GROUP)], out_sems.at[t, h]
            )
            copy.start()
            outgoing.append(copy)
    for copy in outgoing:
        copy.wait()


def unpack_kernel(block_rows, place_ref, back_ref, k_ref, v_ref, o_ref, qg_ref, kg_ref, vg_ref):
    chan = place_ref[0]
    tall = 2 * GROUP
    for tile in range(0, k_ref.shape[0], tall):
        rows = slice(tile, tile + tall)
        bases = [jnp.bitwise_xor(chan, (tile + h * GROUP) // GROUP) * GROUP for h in range(2)]
        for p in range(TURNS):
            conv_out, adjoint = [
                jnp.concatenate(
                    [
                        jnp.swapaxes(back_ref[pl.ds(bases[h], GROUP), a * TURNS + p], 0, 1)
                        for h in range(2)
                    ],
                    axis=1,
                )
                for a in range(2)
            ]
            for m in range(block_rows):
                columns = lanes(m * TURNS + p)
                qg_ref[rows, columns] = (conv_out[m] * o_ref[rows, columns].astype(F32)).astype(BF16)
                kg_ref[rows, columns] = (adjoint[m] * v_ref[rows, columns].astype(F32)).astype(BF16)
                vg_ref[rows, columns] = (adjoint[m] * k_ref[rows, columns].astype(F32)).astype(BF16)


def total_kernel(block_rows, core_ref, *refs):
    grad_ref = refs[-1]
    for other in range(2):
        half = jnp.bitwise_xor(core_ref[0], other)
        for p in range(2):
            total = jnp.swapaxes(refs[other][:, p] + refs[other + 2][:, p], 0, 1)
            for m in range(block_rows):
                start = pl.multiple_of((m * TURNS + 2 * half + p) * INNER, INNER)
                grad_ref[:, pl.ds(start, INNER)] = total[m]


def local_call(kernel, name, out_shape, place, *arrays):
    count = len(arrays)
    specs = in_vmem(count)
    if place is not None:
        specs = [pl.BlockSpec(memory_space=pltpu.SMEM)] + specs
        arrays = (place,) + arrays
    single = not isinstance(out_shape, tuple)
    return pl.pallas_call(
        kernel,
        out_shape=out_shape,
        in_specs=specs,
        out_specs=in_vmem(1)[0] if single else tuple(in_vmem(len(out_shape))),
        compiler_params=pltpu.CompilerParams(vmem_limit_bytes=VMEM_BYTES),
        name=name,
    )(*arrays)


def pack(block_rows, place, arrays):
    slab, width = arrays[0].shape
    shape = (slab, SIGNALS, TURNS, block_rows, INNER)
    return pl.pallas_call(
        functools.partial(pack_kernel, block_rows),
        out_shape=jax.ShapeDtypeStruct(shape, F32),
        in_specs=[pl.BlockSpec(memory_space=pltpu.SMEM)] + [pl.BlockSpec(memory_space=pl.ANY)] * 5,
        out_specs=pl.BlockSpec(memory_space=pl.ANY),
        scratch_shapes=[pltpu.VMEM((slab, width), array.dtype) for array in arrays]
        + [
            pltpu.VMEM(shape, F32),
            pltpu.SemaphoreType.DMA((slab // (2 * GROUP), 5)),
            pltpu.SemaphoreType.DMA((slab // (2 * GROUP), 2)),
        ],
        compiler_params=pltpu.CompilerParams(vmem_limit_bytes=PACK_BYTES),
        name="pack",
    )(place, *arrays)


def shards(query_proj, key_proj, value_proj, out_cotangent, filter_raw):
    slab, width = query_proj.shape
    parts = lax.axis_size("seq")
    groups = lax.axis_size("chan")
    length = parts * width
    scale = 1.0 / (length * math.sqrt(length))
    block_rows = ROWS // parts
    chan = lax.axis_index("chan").astype(jnp.int32)
    core, place = (chan & 1).reshape(1), (chan & 2).reshape(1)

    def exchange(value, distance):
        return lax.ppermute(value, "chan", [(c, c ^ distance) for c in range(groups)])

    sent = pack(
        block_rows, place, (query_proj, key_proj, value_proj, out_cotangent, filter_raw)
    )
    starts = [((chan & 1) ^ k).astype(jnp.uint32) * GROUP for k in range(groups)]
    sent, core, place, starts = lax.optimization_barrier((sent, core, place, starts))
    received = lax.all_to_all(sent, "seq", split_axis=0, concat_axis=0, tiled=True)
    signals = convolve(core, received, scale, lambda value: exchange(value, 1))
    back = lax.all_to_all(signals, "seq", split_axis=0, concat_axis=0, tiled=True)
    pieces = []
    for k in range(groups):
        zero = jnp.uint32(0)
        place_of = (starts[k], jnp.uint32(2 * TURNS), zero, zero)
        piece = lax.dynamic_slice(back, place_of, (GROUP, 2, block_rows, INNER))
        pieces.append(exchange(piece, k) if k > 0 else piece)
    grads = local_call(
        functools.partial(unpack_kernel, block_rows),
        "unpack",
        (jax.ShapeDtypeStruct((slab, width), BF16),) * 3,
        place,
        back,
        key_proj,
        value_proj,
        out_cotangent,
    )
    filter_grad = local_call(
        functools.partial(total_kernel, block_rows),
        "total",
        jax.ShapeDtypeStruct((slab // groups, width), F32),
        core,
        *pieces,
    )
    return (*grads, filter_grad)


def solution(mesh):
    placed = (
        P("chan", "seq"),
        P("chan", "seq"),
        P("chan", "seq"),
        P("chan", "seq"),
        P(None, "seq"),
    )
    return jax.shard_map(
        shards,
        mesh=mesh,
        in_specs=placed,
        out_specs=(P("chan", "seq"), P("chan", "seq"), P("chan", "seq"), P("chan", "seq")),
        check_vma=False,
    )
```

```python
import functools
import itertools
import math

import jax
import jax.numpy as jnp
import ml_dtypes
import numpy as np
from jax import lax
from jax.experimental import pallas as pl
from jax.experimental.pallas import tpu as pltpu
from jax.sharding import PartitionSpec as P

F32 = jnp.float32
BF16 = jnp.bfloat16
SIGNALS = 3
ROWS = 256
TURNS = 4
INNER = 128
CHUNK = 16
GROUP = 8
VMEM_BYTES = 28 * 1024 * 1024
PACK_BYTES = 58 * 1024 * 1024


def halves(table):
    table = table.astype(np.float32)
    high = table.astype(ml_dtypes.bfloat16)
    low = (table - high.astype(np.float32)).astype(ml_dtypes.bfloat16)
    return np.stack([high, low])


def tables(scale):
    width = TURNS * INNER
    k = np.arange(ROWS)[:, None] + 0.25
    angle = 2.0 * np.pi * k * np.arange(ROWS)[None, :] / ROWS
    first = np.concatenate([np.cos(angle), -np.sin(angle)], axis=0)
    turn = 2.0 * np.pi * k * np.arange(width)[None, :] / (ROWS * width)
    turn = np.stack([np.cos(turn), np.sin(turn)]).astype(np.float32)
    l = np.arange(INNER)
    lasts = []
    for j in range(TURNS):
        angle = 2.0 * np.pi * (l[:, None] * (j + TURNS * l[None, :]) % width) / width
        cos, sin = np.cos(angle), np.sin(angle)
        lasts.append(
            np.concatenate(
                [np.concatenate([cos, -sin], axis=1), np.concatenate([sin, cos], axis=1)], axis=0
            )
        )
    last = np.stack(lasts)
    return (
        halves(first),
        halves(first.T),
        turn,
        halves(last),
        halves(last.transpose(0, 2, 1) * scale),
    )


def times(pair, cos, sin):
    return pair[0] * cos - pair[1] * sin, pair[1] * cos + pair[0] * sin


def add(first, second):
    return first[0] + second[0], first[1] + second[1]


def sub(first, second):
    return first[0] - second[0], first[1] - second[1]


def quarter(pair, sign):
    return (-pair[1], pair[0]) if sign > 0 else (pair[1], -pair[0])


def four_point(z, sign):
    s0, d0 = add(z[0], z[2]), sub(z[0], z[2])
    s1, d1 = add(z[1], z[3]), sub(z[1], z[3])
    if sign > 0:
        return [
            add(s0, s1),
            (d0[0] - d1[1], d0[1] + d1[0]),
            sub(s0, s1),
            (d0[0] + d1[1], d0[1] - d1[0]),
        ]
    return [
        add(s0, s1),
        (d0[0] + d1[1], d0[1] - d1[0]),
        sub(s0, s1),
        (d0[0] - d1[1], d0[1] + d1[0]),
    ]


def split(value):
    high = value.astype(BF16)
    return high, (value - high.astype(F32)).astype(BF16)


def dot(first, second):
    return jnp.dot(first, second, preferred_element_type=F32)


def lanes(index):
    return slice(index * INNER, (index + 1) * INNER)


def imag(rows):
    return slice(ROWS + rows.start, ROWS + rows.stop)


def columns(pair):
    return slice(2 * pair * INNER, 2 * (pair + 1) * INNER)


def mix(x_ref, first_ref, mixed_ref, place, first_slot, part):
    data = jnp.concatenate(
        [x_ref[:, first_slot + p].reshape(ROWS, INNER) for p in range(2)], axis=1
    )
    high, low = split(data)
    rows = slice(part * ROWS, (part + 1) * ROWS)
    mixed_ref[rows, place] = (
        dot(first_ref[0, rows], high)
        + dot(first_ref[0, rows], low)
        + dot(first_ref[1, rows], high)
    )


def opening(mixed_ref, turn_ref, z_ref, rows):
    z = []
    for p in range(TURNS):
        cos, sin = turn_ref[0, rows, lanes(p)], turn_ref[1, rows, lanes(p)]
        pair = (mixed_ref[rows, lanes(p)], mixed_ref[imag(rows), lanes(p)])
        z.append(times(pair, cos, -sin))
    z = four_point(z, -1)
    for j in range(TURNS):
        for part in range(2):
            high, low = split(z[j][part])
            z_ref[0, j, rows, lanes(part)] = high
            z_ref[1, j, rows, lanes(part)] = low


def last(z_ref, last_ref, spectra_ref, j):
    high, low = z_ref[0, j], z_ref[1, j]
    spectra_ref[j] = (
        dot(high, last_ref[0, j]) + dot(low, last_ref[0, j]) + dot(high, last_ref[1, j])
    )


def product(one_ref, two_ref, conjugate, product_ref, j, rows):
    one = (one_ref[j, rows, lanes(0)], one_ref[j, rows, lanes(1)])
    two = (two_ref[j, rows, lanes(0)], two_ref[j, rows, lanes(1)])
    pair = times(one, two[0], -two[1] if conjugate else two[1])
    for part in range(2):
        high, low = split(pair[part])
        product_ref[0, j, rows, lanes(part)] = high
        product_ref[1, j, rows, lanes(part)] = low


def closing(u_ref, turn_ref, v_ref, rows):
    z = [(u_ref[j, rows, lanes(0)], u_ref[j, rows, lanes(1)]) for j in range(TURNS)]
    z = four_point(z, 1)
    for p in range(TURNS):
        cos, sin = turn_ref[0, rows, lanes(p)], turn_ref[1, rows, lanes(p)]
        pair = times(z[p], cos, sin)
        for part, place in zip(pair, (rows, imag(rows))):
            high, low = split(part)
            v_ref[0, place, lanes(p)] = high
            v_ref[1, place, lanes(p)] = low


def unmix(v_ref, first_back_ref, store, pair):
    high, low = v_ref[0, :, columns(pair)], v_ref[1, :, columns(pair)]
    out = (
        dot(first_back_ref[0], high)
        + dot(first_back_ref[0], low)
        + dot(first_back_ref[1], high)
    )
    for p in range(2):
        store(2 * pair + p, out[:, lanes(p)])


def steps(function, *ranges):
    return [functools.partial(function, *place) for place in itertools.product(*ranges)]


def interleave(*lines):
    for matrix, vector in lines:
        count = max(len(matrix), 1)
        for i in range(count):
            for step in matrix[i : i + 1]:
                step()
            for step in vector[i * len(vector) // count : (i + 1) * len(vector) // count]:
                step()


CHUNKS = [slice(i, i + CHUNK) for i in range(0, ROWS, CHUNK)]
PAIRS = range(TURNS // 2)
ALL_TURNS = range(TURNS)


def correlate_kernel(
    core_ref,
    x_ref,
    first_ref,
    first_back_ref,
    turn_ref,
    last_ref,
    last_back_ref,
    gated_ref,
    carried_ref,
    kept_ref,
    given_ref,
    mixed_ref,
    z_ref,
    product_ref,
    u_ref,
    v_ref,
    halves_ref,
):
    blocks, _, block_rows, _ = x_ref.shape
    core = core_ref[0]

    def store(p, value):
        halves_ref[p // 2, :, p % 2] = value.reshape(blocks, block_rows, INNER)

    spectra = (gated_ref, carried_ref)
    def mixes(a, pair, part):
        mix(x_ref, first_ref, mixed_ref.at[a], columns(pair), a * TURNS + 2 * pair, part)

    opens = [functools.partial(opening, mixed_ref.at[a], turn_ref, z_ref.at[a]) for a in range(2)]
    lasts = [functools.partial(last, z_ref.at[a], last_ref, spectra[a]) for a in range(2)]
    products = functools.partial(product, carried_ref, gated_ref, True, product_ref)
    last_back = functools.partial(last, product_ref, last_back_ref, u_ref)
    close = functools.partial(closing, u_ref, turn_ref, v_ref)
    interleave(
        (steps(mixes, [0], PAIRS, range(2)), []),
        (steps(mixes, [1], PAIRS, range(2)), steps(opens[0], CHUNKS)),
        (steps(lasts[0], ALL_TURNS), steps(opens[1], CHUNKS)),
        (steps(lasts[1], [0]), []),
        (steps(lasts[1], ALL_TURNS[1:]), steps(products, ALL_TURNS[:-1], CHUNKS)),
        (steps(last_back, ALL_TURNS[:-1]), steps(products, ALL_TURNS[-1:], CHUNKS)),
        (steps(last_back, ALL_TURNS[-1:]), []),
        ([], steps(close, CHUNKS)),
        (steps(functools.partial(unmix, v_ref, first_back_ref, store), PAIRS), []),
    )
    kept_ref[...] = halves_ref[core]
    given_ref[...] = halves_ref[1 - core]


def convolve_kernel(
    core_ref,
    x_ref,
    other_ref,
    gated_ref,
    carried_ref,
    first_ref,
    first_back_ref,
    turn_ref,
    last_ref,
    last_back_ref,
    conv_ref,
    v_ref,
    mixed_ref,
    z_ref,
    filter_ref,
    product_ref,
    u_ref,
    v_conv_ref,
):
    blocks, _, block_rows, _ = x_ref.shape
    wide = 2 * INNER

    def store(p, value):
        conv_ref[:, p] = value.reshape(blocks, block_rows, INNER)

    v_refs = (v_conv_ref, v_ref)

    def mixes(other, part):
        start = pl.multiple_of(jnp.bitwise_xor(core_ref[0], other) * wide, wide)
        source, first_slot = ((x_ref, 2 * TURNS), (other_ref, 0))[other]
        mix(source, first_ref, mixed_ref, pl.ds(start, wide), first_slot, part)

    opens = functools.partial(opening, mixed_ref, turn_ref, z_ref)
    lasts = functools.partial(last, z_ref, last_ref, filter_ref)

    def products(j, rows):
        product(gated_ref, filter_ref, False, product_ref.at[0], j, rows)
        product(carried_ref, filter_ref, True, product_ref.at[1], j, rows)

    def last_back(j, a):
        last(product_ref.at[a], last_back_ref, u_ref.at[a], j)

    close = [
        functools.partial(closing, u_ref.at[a], turn_ref, v_refs[a]) for a in range(2)
    ]
    interleave(
        (steps(mixes, range(2), range(2)), []),
        ([], steps(opens, CHUNKS)),
        (steps(lasts, [0]), []),
        (steps(lasts, ALL_TURNS[1:]), steps(products, ALL_TURNS[:-1], CHUNKS)),
        (steps(last_back, ALL_TURNS[:-1], range(2)), steps(products, ALL_TURNS[-1:], CHUNKS)),
        (steps(last_back, ALL_TURNS[-1:], [0]), []),
        (steps(last_back, ALL_TURNS[-1:], [1]), steps(close[0], CHUNKS)),
        (
            steps(functools.partial(unmix, v_conv_ref, first_back_ref, store), PAIRS),
            steps(close[1], CHUNKS),
        ),
    )


def gather_kernel(conv_ref, v_ref, first_back_ref, kept_ref, taken_ref, out_ref):
    blocks, _, block_rows, _ = conv_ref.shape

    def store(p, value):
        out_ref[:, TURNS + p] = value.reshape(blocks, block_rows, INNER)

    def rest(p):
        out_ref[:, p] = conv_ref[:, p]
        if p < 2:
            out_ref[:, 2 * TURNS + p] = kept_ref[:, p] + taken_ref[:, p]

    interleave(
        (steps(functools.partial(unmix, v_ref, first_back_ref, store), PAIRS), steps(rest, ALL_TURNS))
    )


def in_vmem(count):
    return [pl.BlockSpec(memory_space=pltpu.VMEM)] * count


def convolve(core, received, scale, exchange):
    first, first_back, turn, last_table, last_back = [
        jnp.asarray(table) for table in tables(scale)
    ]
    width = TURNS * INNER
    blocks, _, block_rows, _ = received.shape
    other_filter = exchange(received[:, 2 * TURNS :])
    spectrum = (TURNS, ROWS, 2 * INNER)
    two_halves = jax.ShapeDtypeStruct((blocks, 2, block_rows, INNER), F32)
    params = pltpu.CompilerParams(vmem_limit_bytes=VMEM_BYTES)
    gated, carried, kept, given = pl.pallas_call(
        correlate_kernel,
        out_shape=(jax.ShapeDtypeStruct(spectrum, F32),) * 2 + (two_halves,) * 2,
        in_specs=[pl.BlockSpec(memory_space=pltpu.SMEM)] + in_vmem(6),
        out_specs=tuple(in_vmem(4)),
        scratch_shapes=[
            pltpu.VMEM((2, 2 * ROWS, width), F32),
            pltpu.VMEM((2, 2, *spectrum), BF16),
            pltpu.VMEM((2, *spectrum), BF16),
            pltpu.VMEM(spectrum, F32),
            pltpu.VMEM((2, 2 * ROWS, width), BF16),
            pltpu.VMEM((2, *two_halves.shape), F32),
        ],
        compiler_params=params,
        name="correlate",
    )(core, received, first, first_back, turn, last_table, last_back)
    taken = exchange(given)
    conv_out, mixed_adjoint = pl.pallas_call(
        convolve_kernel,
        out_shape=(
            jax.ShapeDtypeStruct((blocks, TURNS, block_rows, INNER), F32),
            jax.ShapeDtypeStruct((2, 2 * ROWS, width), BF16),
        ),
        in_specs=[pl.BlockSpec(memory_space=pltpu.SMEM)] + in_vmem(9),
        out_specs=tuple(in_vmem(2)),
        scratch_shapes=[
            pltpu.VMEM((2 * ROWS, width), F32),
            pltpu.VMEM((2, *spectrum), BF16),
            pltpu.VMEM(spectrum, F32),
            pltpu.VMEM((2, 2, *spectrum), BF16),
            pltpu.VMEM((2, *spectrum), F32),
            pltpu.VMEM((2, 2 * ROWS, width), BF16),
        ],
        compiler_params=params,
        name="convolve",
    )(core, received, other_filter, gated, carried, first, first_back, turn, last_table, last_back)
    return pl.pallas_call(
        gather_kernel,
        out_shape=jax.ShapeDtypeStruct((blocks, 2 * TURNS + 2, block_rows, INNER), F32),
        in_specs=in_vmem(5),
        out_specs=in_vmem(1)[0],
        compiler_params=params,
        name="gather",
    )(conv_out, mixed_adjoint, first_back, kept, taken)


def pack_kernel(block_rows, place_ref, core_ref, *refs):
    sources, sent_ref, held, built, sems, out_sems = refs[:5], refs[5], refs[6:11], *refs[11:]
    chan = place_ref[0]
    tall = 2 * GROUP
    tiles = range(0, sources[0].shape[0], tall)
    copies = []
    for t, tile in enumerate(tiles):
        for n in range(5):
            rows = pl.ds(tile, tall)
            copies.append(pltpu.make_async_copy(sources[n].at[rows], held[n].at[rows], sems.at[t, n]))
    for copy in copies:
        copy.start()
    outgoing = []
    q_ref, k_ref, v_ref, o_ref, f_ref = held
    for t, tile in enumerate(tiles):
        for copy in copies[5 * t : 5 * t + 5]:
            copy.wait()
        rows = slice(tile, tile + tall)
        for p in range(TURNS):
            values = [[], [], []]
            half = 2 * core_ref[0] + p
            for m in range(block_rows):
                columns = lanes(m * TURNS + p)
                values[0].append(k_ref[rows, columns].astype(F32) * v_ref[rows, columns].astype(F32))
                values[1].append(q_ref[rows, columns].astype(F32) * o_ref[rows, columns].astype(F32))
                if p < 2:
                    start = pl.multiple_of((m * TURNS + half) * INNER, INNER)
                    values[2].append(f_ref[rows, pl.ds(start, INNER)])
            for h in range(2):
                for a in range(SIGNALS if p < 2 else 2):
                    block = jnp.stack([value[h * GROUP : (h + 1) * GROUP] for value in values[a]])
                    start = tile + h * GROUP
                    built[start : start + GROUP, a * TURNS + p] = jnp.swapaxes(block, 0, 1)
        for h in range(2):
            start = tile + h * GROUP
            target = jnp.bitwise_xor(chan, start // GROUP) * GROUP
            copy = pltpu.make_async_copy(
                built.at[pl.ds(start, GROUP)], sent_ref.at[pl.ds(target, GROUP)], out_sems.at[t, h]
            )
            copy.start()
            outgoing.append(copy)
    for copy in outgoing:
        copy.wait()


def unpack_kernel(block_rows, place_ref, back_ref, k_ref, v_ref, o_ref, qg_ref, kg_ref, vg_ref):
    chan = place_ref[0]
    tall = 2 * GROUP
    for tile in range(0, k_ref.shape[0], tall):
        rows = slice(tile, tile + tall)
        bases = [jnp.bitwise_xor(chan, (tile + h * GROUP) // GROUP) * GROUP for h in range(2)]
        for p in range(TURNS):
            conv_out, adjoint = [
                jnp.concatenate(
                    [
                        jnp.swapaxes(back_ref[pl.ds(bases[h], GROUP), a * TURNS + p], 0, 1)
                        for h in range(2)
                    ],
                    axis=1,
                )
                for a in range(2)
            ]
            for m in range(block_rows):
                columns = lanes(m * TURNS + p)
                qg_ref[rows, columns] = (conv_out[m] * o_ref[rows, columns].astype(F32)).astype(BF16)
                kg_ref[rows, columns] = (adjoint[m] * v_ref[rows, columns].astype(F32)).astype(BF16)
                vg_ref[rows, columns] = (adjoint[m] * k_ref[rows, columns].astype(F32)).astype(BF16)


def total_kernel(block_rows, core_ref, *refs):
    grad_ref = refs[-1]
    for other in range(2):
        half = jnp.bitwise_xor(core_ref[0], other)
        for p in range(2):
            total = jnp.swapaxes(refs[other][:, p] + refs[other + 2][:, p], 0, 1)
            for m in range(block_rows):
                start = pl.multiple_of((m * TURNS + 2 * half + p) * INNER, INNER)
                grad_ref[:, pl.ds(start, INNER)] = total[m]


def local_call(kernel, name, out_shape, place, *arrays):
    count = len(arrays)
    specs = in_vmem(count)
    if place is not None:
        specs = [pl.BlockSpec(memory_space=pltpu.SMEM)] + specs
        arrays = (place,) + arrays
    single = not isinstance(out_shape, tuple)
    return pl.pallas_call(
        kernel,
        out_shape=out_shape,
        in_specs=specs,
        out_specs=in_vmem(1)[0] if single else tuple(in_vmem(len(out_shape))),
        compiler_params=pltpu.CompilerParams(vmem_limit_bytes=VMEM_BYTES),
        name=name,
    )(*arrays)


def pack(block_rows, place, core, arrays):
    slab, width = arrays[0].shape
    shape = (slab, 2 * TURNS + 2, block_rows, INNER)
    return pl.pallas_call(
        functools.partial(pack_kernel, block_rows),
        out_shape=jax.ShapeDtypeStruct(shape, F32),
        in_specs=[pl.BlockSpec(memory_space=pltpu.SMEM)] * 2
        + [pl.BlockSpec(memory_space=pl.ANY)] * 5,
        out_specs=pl.BlockSpec(memory_space=pl.ANY),
        scratch_shapes=[pltpu.VMEM((slab, width), array.dtype) for array in arrays]
        + [
            pltpu.VMEM(shape, F32),
            pltpu.SemaphoreType.DMA((slab // (2 * GROUP), 5)),
            pltpu.SemaphoreType.DMA((slab // (2 * GROUP), 2)),
        ],
        compiler_params=pltpu.CompilerParams(vmem_limit_bytes=PACK_BYTES),
        name="pack",
    )(place, core, *arrays)


def shards(query_proj, key_proj, value_proj, out_cotangent, filter_raw):
    slab, width = query_proj.shape
    parts = lax.axis_size("seq")
    groups = lax.axis_size("chan")
    length = parts * width
    scale = 1.0 / (length * math.sqrt(length))
    block_rows = ROWS // parts
    chan = lax.axis_index("chan").astype(jnp.int32)
    core, place = (chan & 1).reshape(1), (chan & 2).reshape(1)

    def exchange(value, distance):
        return lax.ppermute(value, "chan", [(c, c ^ distance) for c in range(groups)])

    sent = pack(
        block_rows, place, core, (query_proj, key_proj, value_proj, out_cotangent, filter_raw)
    )
    starts = [((chan & 1) ^ k).astype(jnp.uint32) * GROUP for k in range(groups)]
    sent, core, place, starts = lax.optimization_barrier((sent, core, place, starts))
    received = lax.all_to_all(sent, "seq", split_axis=0, concat_axis=0, tiled=True)
    signals = convolve(core, received, scale, lambda value: exchange(value, 1))
    back = lax.all_to_all(signals, "seq", split_axis=0, concat_axis=0, tiled=True)
    pieces = []
    for k in range(groups):
        zero = jnp.uint32(0)
        place_of = (starts[k], jnp.uint32(2 * TURNS), zero, zero)
        piece = lax.dynamic_slice(back, place_of, (GROUP, 2, block_rows, INNER))
        pieces.append(exchange(piece, k) if k > 0 else piece)
    grads = local_call(
        functools.partial(unpack_kernel, block_rows),
        "unpack",
        (jax.ShapeDtypeStruct((slab, width), BF16),) * 3,
        place,
        back,
        key_proj,
        value_proj,
        out_cotangent,
    )
    filter_grad = local_call(
        functools.partial(total_kernel, block_rows),
        "total",
        jax.ShapeDtypeStruct((slab // groups, width), F32),
        core,
        *pieces,
    )
    return (*grads, filter_grad)


def solution(mesh):
    placed = (
        P("chan", "seq"),
        P("chan", "seq"),
        P("chan", "seq"),
        P("chan", "seq"),
        P(None, "seq"),
    )
    return jax.shard_map(
        shards,
        mesh=mesh,
        in_specs=placed,
        out_specs=(P("chan", "seq"), P("chan", "seq"), P("chan", "seq"), P("chan", "seq")),
        check_vma=False,
    )
```

```python
import functools
import itertools
import math

import jax
import jax.numpy as jnp
import ml_dtypes
import numpy as np
from jax import lax
from jax.experimental import pallas as pl
from jax.experimental.pallas import tpu as pltpu
from jax.sharding import PartitionSpec as P

F32 = jnp.float32
BF16 = jnp.bfloat16
SIGNALS = 3
ROWS = 256
TURNS = 4
INNER = 128
CHUNK = 16
GROUP = 8
VMEM_BYTES = 28 * 1024 * 1024
PACK_BYTES = 58 * 1024 * 1024


def halves(table):
    table = table.astype(np.float32)
    high = table.astype(ml_dtypes.bfloat16)
    low = (table - high.astype(np.float32)).astype(ml_dtypes.bfloat16)
    return np.stack([high, low])


def tables(scale):
    width = TURNS * INNER
    k = np.arange(ROWS)[:, None] + 0.25
    angle = 2.0 * np.pi * k * np.arange(ROWS)[None, :] / ROWS
    first = np.concatenate([np.cos(angle), -np.sin(angle)], axis=0)
    turn = 2.0 * np.pi * k * np.arange(width)[None, :] / (ROWS * width)
    turn = np.stack([np.cos(turn), np.sin(turn)]).astype(np.float32)
    l = np.arange(INNER)
    lasts = []
    for j in range(TURNS):
        angle = 2.0 * np.pi * (l[:, None] * (j + TURNS * l[None, :]) % width) / width
        cos, sin = np.cos(angle), np.sin(angle)
        lasts.append(
            np.concatenate(
                [np.concatenate([cos, -sin], axis=1), np.concatenate([sin, cos], axis=1)], axis=0
            )
        )
    last = np.stack(lasts)
    return (
        halves(first),
        halves(first.T),
        turn,
        halves(last),
        halves(last.transpose(0, 2, 1) * scale),
    )


def times(pair, cos, sin):
    return pair[0] * cos - pair[1] * sin, pair[1] * cos + pair[0] * sin


def add(first, second):
    return first[0] + second[0], first[1] + second[1]


def sub(first, second):
    return first[0] - second[0], first[1] - second[1]


def quarter(pair, sign):
    return (-pair[1], pair[0]) if sign > 0 else (pair[1], -pair[0])


def four_point(z, sign):
    s0, d0 = add(z[0], z[2]), sub(z[0], z[2])
    s1, d1 = add(z[1], z[3]), sub(z[1], z[3])
    if sign > 0:
        return [
            add(s0, s1),
            (d0[0] - d1[1], d0[1] + d1[0]),
            sub(s0, s1),
            (d0[0] + d1[1], d0[1] - d1[0]),
        ]
    return [
        add(s0, s1),
        (d0[0] + d1[1], d0[1] - d1[0]),
        sub(s0, s1),
        (d0[0] - d1[1], d0[1] + d1[0]),
    ]


def split(value):
    high = value.astype(BF16)
    return high, (value - high.astype(F32)).astype(BF16)


def dot(first, second):
    return jnp.dot(first, second, preferred_element_type=F32)


def lanes(index):
    return slice(index * INNER, (index + 1) * INNER)


def imag(rows):
    return slice(ROWS + rows.start, ROWS + rows.stop)


def columns(pair):
    return slice(2 * pair * INNER, 2 * (pair + 1) * INNER)


def mix(x_ref, first_ref, mixed_ref, place, first_slot, part):
    data = jnp.concatenate(
        [x_ref[:, first_slot + p].reshape(ROWS, INNER) for p in range(2)], axis=1
    )
    high, low = split(data)
    rows = slice(part * ROWS, (part + 1) * ROWS)
    mixed_ref[rows, place] = (
        dot(first_ref[0, rows], high)
        + dot(first_ref[0, rows], low)
        + dot(first_ref[1, rows], high)
    )


def opening(mixed_ref, turn_ref, z_ref, rows):
    z = []
    for p in range(TURNS):
        cos, sin = turn_ref[0, rows, lanes(p)], turn_ref[1, rows, lanes(p)]
        pair = (mixed_ref[rows, lanes(p)], mixed_ref[imag(rows), lanes(p)])
        z.append(times(pair, cos, -sin))
    z = four_point(z, -1)
    for j in range(TURNS):
        for part in range(2):
            high, low = split(z[j][part])
            z_ref[0, j, rows, lanes(part)] = high
            z_ref[1, j, rows, lanes(part)] = low


def last(z_ref, last_ref, spectra_ref, j):
    high, low = z_ref[0, j], z_ref[1, j]
    spectra_ref[j] = (
        dot(high, last_ref[0, j]) + dot(low, last_ref[0, j]) + dot(high, last_ref[1, j])
    )


def product(one_ref, two_ref, conjugate, product_ref, j, rows):
    one = (one_ref[j, rows, lanes(0)], one_ref[j, rows, lanes(1)])
    two = (two_ref[j, rows, lanes(0)], two_ref[j, rows, lanes(1)])
    pair = times(one, two[0], -two[1] if conjugate else two[1])
    for part in range(2):
        high, low = split(pair[part])
        product_ref[0, j, rows, lanes(part)] = high
        product_ref[1, j, rows, lanes(part)] = low


def closing(u_ref, turn_ref, v_ref, rows):
    z = [(u_ref[j, rows, lanes(0)], u_ref[j, rows, lanes(1)]) for j in range(TURNS)]
    z = four_point(z, 1)
    for p in range(TURNS):
        cos, sin = turn_ref[0, rows, lanes(p)], turn_ref[1, rows, lanes(p)]
        pair = times(z[p], cos, sin)
        for part, place in zip(pair, (rows, imag(rows))):
            high, low = split(part)
            v_ref[0, place, lanes(p)] = high
            v_ref[1, place, lanes(p)] = low


def unmix(v_ref, first_back_ref, store, pair):
    high, low = v_ref[0, :, columns(pair)], v_ref[1, :, columns(pair)]
    out = (
        dot(first_back_ref[0], high)
        + dot(first_back_ref[0], low)
        + dot(first_back_ref[1], high)
    )
    for p in range(2):
        store(2 * pair + p, out[:, lanes(p)])


def steps(function, *ranges):
    return [functools.partial(function, *place) for place in itertools.product(*ranges)]


def interleave(*lines):
    for matrix, vector in lines:
        count = max(len(matrix), 1)
        for i in range(count):
            for step in matrix[i : i + 1]:
                step()
            for step in vector[i * len(vector) // count : (i + 1) * len(vector) // count]:
                step()


CHUNKS = [slice(i, i + CHUNK) for i in range(0, ROWS, CHUNK)]
PAIRS = range(TURNS // 2)
ALL_TURNS = range(TURNS)


def correlate_kernel(
    core_ref,
    x_ref,
    first_ref,
    first_back_ref,
    turn_ref,
    last_ref,
    last_back_ref,
    gated_ref,
    carried_ref,
    kept_ref,
    given_ref,
    own_ref,
    mixed_ref,
    z_ref,
    product_ref,
    u_ref,
    v_ref,
    halves_ref,
):
    blocks, _, block_rows, _ = x_ref.shape
    core = core_ref[0]

    def store(p, value):
        halves_ref[p // 2, :, p % 2] = value.reshape(blocks, block_rows, INNER)

    def mix_own(part):
        mix(x_ref, first_ref, own_ref, slice(None), 2 * TURNS, part)

    spectra = (gated_ref, carried_ref)
    def mixes(a, pair, part):
        mix(x_ref, first_ref, mixed_ref.at[a], columns(pair), a * TURNS + 2 * pair, part)

    opens = [functools.partial(opening, mixed_ref.at[a], turn_ref, z_ref.at[a]) for a in range(2)]
    lasts = [functools.partial(last, z_ref.at[a], last_ref, spectra[a]) for a in range(2)]
    products = functools.partial(product, carried_ref, gated_ref, True, product_ref)
    last_back = functools.partial(last, product_ref, last_back_ref, u_ref)
    close = functools.partial(closing, u_ref, turn_ref, v_ref)
    interleave(
        (steps(mixes, [0], PAIRS, range(2)), []),
        (steps(mixes, [1], PAIRS, range(2)), steps(opens[0], CHUNKS)),
        (steps(lasts[0], ALL_TURNS), steps(opens[1], CHUNKS)),
        (steps(lasts[1], [0]), []),
        (steps(lasts[1], ALL_TURNS[1:]), steps(products, ALL_TURNS[:-1], CHUNKS)),
        (steps(last_back, ALL_TURNS[:-1]), steps(products, ALL_TURNS[-1:], CHUNKS)),
        (steps(last_back, ALL_TURNS[-1:]), []),
        (steps(mix_own, range(2)), steps(close, CHUNKS)),
        (steps(functools.partial(unmix, v_ref, first_back_ref, store), PAIRS), []),
    )
    kept_ref[...] = halves_ref[core]
    given_ref[...] = halves_ref[1 - core]


def convolve_kernel(
    core_ref,
    own_ref,
    other_ref,
    gated_ref,
    carried_ref,
    first_ref,
    first_back_ref,
    turn_ref,
    last_ref,
    last_back_ref,
    conv_ref,
    v_ref,
    mixed_ref,
    z_ref,
    filter_ref,
    product_ref,
    u_ref,
    v_conv_ref,
):
    blocks, _, block_rows, _ = other_ref.shape
    wide = 2 * INNER

    def place(other):
        start = jnp.bitwise_xor(core_ref[0], other) * wide
        return pl.ds(pl.multiple_of(start, wide), wide)

    def store(p, value):
        conv_ref[:, p] = value.reshape(blocks, block_rows, INNER)

    def mix_other(part):
        mix(other_ref, first_ref, mixed_ref, place(1), 0, part)

    def copy_own(part):
        rows = slice(part * ROWS, (part + 1) * ROWS)
        mixed_ref[rows, place(0)] = own_ref[rows]

    v_refs = (v_conv_ref, v_ref)
    opens = functools.partial(opening, mixed_ref, turn_ref, z_ref)

    def lasts(part, j):
        rows = slice(part * ROWS // 2, (part + 1) * ROWS // 2)
        last(z_ref.at[:, :, rows], last_ref, filter_ref.at[:, rows], j)

    def products(j, rows):
        product(gated_ref, filter_ref, False, product_ref.at[0], j, rows)
        product(carried_ref, filter_ref, True, product_ref.at[1], j, rows)

    def last_back(j, a):
        last(product_ref.at[a], last_back_ref, u_ref.at[a], j)

    close = [
        functools.partial(closing, u_ref.at[a], turn_ref, v_refs[a]) for a in range(2)
    ]
    interleave(
        (steps(mix_other, range(2)), steps(copy_own, range(2))),
        ([], steps(opens, CHUNKS[: len(CHUNKS) // 2])),
        (steps(lasts, [0], ALL_TURNS), steps(opens, CHUNKS[len(CHUNKS) // 2 :])),
        (steps(lasts, [1], [0]), []),
        (steps(lasts, [1], ALL_TURNS[1:]), steps(products, ALL_TURNS[:-1], CHUNKS)),
        (steps(last_back, ALL_TURNS[:-1], range(2)), steps(products, ALL_TURNS[-1:], CHUNKS)),
        (steps(last_back, ALL_TURNS[-1:], [0]), []),
        (steps(last_back, ALL_TURNS[-1:], [1]), steps(close[0], CHUNKS)),
        (
            steps(functools.partial(unmix, v_conv_ref, first_back_ref, store), PAIRS),
            steps(close[1], CHUNKS),
        ),
    )


def gather_kernel(conv_ref, v_ref, first_back_ref, kept_ref, taken_ref, out_ref):
    blocks, _, block_rows, _ = conv_ref.shape

    def store(p, value):
        out_ref[:, TURNS + p] = value.reshape(blocks, block_rows, INNER)

    def rest(p):
        out_ref[:, p] = conv_ref[:, p]
        if p < 2:
            out_ref[:, 2 * TURNS + p] = kept_ref[:, p] + taken_ref[:, p]

    interleave(
        (steps(functools.partial(unmix, v_ref, first_back_ref, store), PAIRS), steps(rest, ALL_TURNS))
    )


def in_vmem(count):
    return [pl.BlockSpec(memory_space=pltpu.VMEM)] * count


def convolve(core, received, scale, exchange):
    first, first_back, turn, last_table, last_back = [
        jnp.asarray(table) for table in tables(scale)
    ]
    width = TURNS * INNER
    blocks, _, block_rows, _ = received.shape
    other_filter = exchange(received[:, 2 * TURNS :])
    spectrum = (TURNS, ROWS, 2 * INNER)
    two_halves = jax.ShapeDtypeStruct((blocks, 2, block_rows, INNER), F32)
    params = pltpu.CompilerParams(vmem_limit_bytes=VMEM_BYTES)
    gated, carried, kept, given, own = pl.pallas_call(
        correlate_kernel,
        out_shape=(jax.ShapeDtypeStruct(spectrum, F32),) * 2 + (two_halves,) * 2
        + (jax.ShapeDtypeStruct((2 * ROWS, 2 * INNER), F32),),
        in_specs=[pl.BlockSpec(memory_space=pltpu.SMEM)] + in_vmem(6),
        out_specs=tuple(in_vmem(5)),
        scratch_shapes=[
            pltpu.VMEM((2, 2 * ROWS, width), F32),
            pltpu.VMEM((2, 2, *spectrum), BF16),
            pltpu.VMEM((2, *spectrum), BF16),
            pltpu.VMEM(spectrum, F32),
            pltpu.VMEM((2, 2 * ROWS, width), BF16),
            pltpu.VMEM((2, *two_halves.shape), F32),
        ],
        compiler_params=params,
        name="correlate",
    )(core, received, first, first_back, turn, last_table, last_back)
    taken = exchange(given)
    conv_out, mixed_adjoint = pl.pallas_call(
        convolve_kernel,
        out_shape=(
            jax.ShapeDtypeStruct((blocks, TURNS, block_rows, INNER), F32),
            jax.ShapeDtypeStruct((2, 2 * ROWS, width), BF16),
        ),
        in_specs=[pl.BlockSpec(memory_space=pltpu.SMEM)] + in_vmem(9),
        out_specs=tuple(in_vmem(2)),
        scratch_shapes=[
            pltpu.VMEM((2 * ROWS, width), F32),
            pltpu.VMEM((2, *spectrum), BF16),
            pltpu.VMEM(spectrum, F32),
            pltpu.VMEM((2, 2, *spectrum), BF16),
            pltpu.VMEM((2, *spectrum), F32),
            pltpu.VMEM((2, 2 * ROWS, width), BF16),
        ],
        compiler_params=params,
        name="convolve",
    )(core, own, other_filter, gated, carried, first, first_back, turn, last_table, last_back)
    return pl.pallas_call(
        gather_kernel,
        out_shape=jax.ShapeDtypeStruct((blocks, 2 * TURNS + 2, block_rows, INNER), F32),
        in_specs=in_vmem(5),
        out_specs=in_vmem(1)[0],
        compiler_params=params,
        name="gather",
    )(conv_out, mixed_adjoint, first_back, kept, taken)


def pack_kernel(block_rows, place_ref, core_ref, *refs):
    sources, sent_ref, held, built, sems, out_sems = refs[:5], refs[5], refs[6:11], *refs[11:]
    chan = place_ref[0]
    tall = 2 * GROUP
    tiles = range(0, sources[0].shape[0], tall)
    needs = ((1, 2), (0, 3), (4,))
    copies = {}
    for t, tile in enumerate(tiles):
        for n in itertools.chain(*needs):
            rows = pl.ds(tile, tall)
            copies[t, n] = pltpu.make_async_copy(sources[n].at[rows], held[n].at[rows], sems.at[t, n])
            copies[t, n].start()
    outgoing = []
    q_ref, k_ref, v_ref, o_ref, f_ref = held
    for t, tile in enumerate(tiles):
        rows = slice(tile, tile + tall)
        for a in range(SIGNALS):
            for n in needs[a]:
                copies[t, n].wait()
            count = TURNS if a < 2 else 2
            for p in range(count):
                values = []
                for m in range(block_rows):
                    columns = lanes(m * TURNS + p)
                    if a == 0:
                        value = k_ref[rows, columns].astype(F32) * v_ref[rows, columns].astype(F32)
                    elif a == 1:
                        value = q_ref[rows, columns].astype(F32) * o_ref[rows, columns].astype(F32)
                    else:
                        start = pl.multiple_of((m * TURNS + 2 * core_ref[0] + p) * INNER, INNER)
                        value = f_ref[rows, pl.ds(start, INNER)]
                    values.append(value)
                for h in range(2):
                    block = jnp.stack([value[h * GROUP : (h + 1) * GROUP] for value in values])
                    start = tile + h * GROUP
                    built[start : start + GROUP, a * TURNS + p] = jnp.swapaxes(block, 0, 1)
            for h in range(2):
                start = tile + h * GROUP
                target = jnp.bitwise_xor(chan, start // GROUP) * GROUP
                slots = pl.ds(a * TURNS, count)
                copy = pltpu.make_async_copy(
                    built.at[pl.ds(start, GROUP), slots],
                    sent_ref.at[pl.ds(target, GROUP), slots],
                    out_sems.at[t, a, h],
                )
                copy.start()
                outgoing.append(copy)
    for copy in outgoing:
        copy.wait()


def unpack_kernel(block_rows, place_ref, back_ref, k_ref, v_ref, o_ref, qg_ref, kg_ref, vg_ref):
    chan = place_ref[0]
    tall = 2 * GROUP
    for tile in range(0, k_ref.shape[0], tall):
        rows = slice(tile, tile + tall)
        bases = [jnp.bitwise_xor(chan, (tile + h * GROUP) // GROUP) * GROUP for h in range(2)]
        for p in range(TURNS):
            conv_out, adjoint = [
                jnp.concatenate(
                    [
                        jnp.swapaxes(back_ref[pl.ds(bases[h], GROUP), a * TURNS + p], 0, 1)
                        for h in range(2)
                    ],
                    axis=1,
                )
                for a in range(2)
            ]
            for m in range(block_rows):
                columns = lanes(m * TURNS + p)
                qg_ref[rows, columns] = (conv_out[m] * o_ref[rows, columns].astype(F32)).astype(BF16)
                kg_ref[rows, columns] = (adjoint[m] * v_ref[rows, columns].astype(F32)).astype(BF16)
                vg_ref[rows, columns] = (adjoint[m] * k_ref[rows, columns].astype(F32)).astype(BF16)


def total_kernel(block_rows, core_ref, *refs):
    grad_ref = refs[-1]
    for other in range(2):
        half = jnp.bitwise_xor(core_ref[0], other)
        for p in range(2):
            total = jnp.swapaxes(refs[other][:, p] + refs[other + 2][:, p], 0, 1)
            for m in range(block_rows):
                start = pl.multiple_of((m * TURNS + 2 * half + p) * INNER, INNER)
                grad_ref[:, pl.ds(start, INNER)] = total[m]


def local_call(kernel, name, out_shape, place, *arrays):
    count = len(arrays)
    specs = in_vmem(count)
    if place is not None:
        specs = [pl.BlockSpec(memory_space=pltpu.SMEM)] + specs
        arrays = (place,) + arrays
    single = not isinstance(out_shape, tuple)
    return pl.pallas_call(
        kernel,
        out_shape=out_shape,
        in_specs=specs,
        out_specs=in_vmem(1)[0] if single else tuple(in_vmem(len(out_shape))),
        compiler_params=pltpu.CompilerParams(vmem_limit_bytes=VMEM_BYTES),
        name=name,
    )(*arrays)


def pack(block_rows, place, core, arrays):
    slab, width = arrays[0].shape
    shape = (slab, 2 * TURNS + 2, block_rows, INNER)
    return pl.pallas_call(
        functools.partial(pack_kernel, block_rows),
        out_shape=jax.ShapeDtypeStruct(shape, F32),
        in_specs=[pl.BlockSpec(memory_space=pltpu.SMEM)] * 2
        + [pl.BlockSpec(memory_space=pl.ANY)] * 5,
        out_specs=pl.BlockSpec(memory_space=pl.ANY),
        scratch_shapes=[pltpu.VMEM((slab, width), array.dtype) for array in arrays]
        + [
            pltpu.VMEM(shape, F32),
            pltpu.SemaphoreType.DMA((slab // (2 * GROUP), 5)),
            pltpu.SemaphoreType.DMA((slab // (2 * GROUP), SIGNALS, 2)),
        ],
        compiler_params=pltpu.CompilerParams(vmem_limit_bytes=PACK_BYTES),
        name="pack",
    )(place, core, *arrays)


def shards(query_proj, key_proj, value_proj, out_cotangent, filter_raw):
    slab, width = query_proj.shape
    parts = lax.axis_size("seq")
    groups = lax.axis_size("chan")
    length = parts * width
    scale = 1.0 / (length * math.sqrt(length))
    block_rows = ROWS // parts
    chan = lax.axis_index("chan").astype(jnp.int32)
    core, place = (chan & 1).reshape(1), (chan & 2).reshape(1)

    def exchange(value, distance):
        return lax.ppermute(value, "chan", [(c, c ^ distance) for c in range(groups)])

    sent = pack(
        block_rows, place, core, (query_proj, key_proj, value_proj, out_cotangent, filter_raw)
    )
    starts = [((chan & 1) ^ k).astype(jnp.uint32) * GROUP for k in range(groups)]
    sent, core, place, starts = lax.optimization_barrier((sent, core, place, starts))
    received = lax.all_to_all(sent, "seq", split_axis=0, concat_axis=0, tiled=True)
    signals = convolve(core, received, scale, lambda value: exchange(value, 1))
    back = lax.all_to_all(signals, "seq", split_axis=0, concat_axis=0, tiled=True)
    pieces = []
    for k in range(groups):
        zero = jnp.uint32(0)
        place_of = (starts[k], jnp.uint32(2 * TURNS), zero, zero)
        piece = lax.dynamic_slice(back, place_of, (GROUP, 2, block_rows, INNER))
        pieces.append(exchange(piece, k) if k > 0 else piece)
    grads = local_call(
        functools.partial(unpack_kernel, block_rows),
        "unpack",
        (jax.ShapeDtypeStruct((slab, width), BF16),) * 3,
        place,
        back,
        key_proj,
        value_proj,
        out_cotangent,
    )
    filter_grad = local_call(
        functools.partial(total_kernel, block_rows),
        "total",
        jax.ShapeDtypeStruct((slab // groups, width), F32),
        core,
        *pieces,
    )
    return (*grads, filter_grad)


def solution(mesh):
    placed = (
        P("chan", "seq"),
        P("chan", "seq"),
        P("chan", "seq"),
        P("chan", "seq"),
        P(None, "seq"),
    )
    return jax.shard_map(
        shards,
        mesh=mesh,
        in_specs=placed,
        out_specs=(P("chan", "seq"), P("chan", "seq"), P("chan", "seq"), P("chan", "seq")),
        check_vma=False,
    )
```
